256 devices in a mesh: row: 8 (over x, core), col: 32 (over z, y).
Axes of the slice: x: 4, y: 4, z: 8, core: 2. Of those that a mesh axis runs over, the one named last changes fastest.
Arguments:
- matrix: float32 [24576, 24576], P('row', 'col'), may hold values from -6 to 6
Outputs:
- y_block: float32 [4, 24576], P(None, 'row')
- reflectors: float32 [4, 24576], P(None, 'row')
- t_factor: float32 [4, 4], replicated
The draws below stay inside these ranges and needn't reach their ends.
All inputs are finite; a program needn't handle non-finite values.
Results may differ from the reference program's by a relative error of at most 0.0003.
Values sent between devices are 32-bit elements; how exact they have to be, the bound alone decides.
No kernel may reach another device: no remote copies, remote signals or barrier semaphores. Data moves between devices by JAX's collectives and lax.ppermute only.
A program may use at most 64 MiB of HBM per device.

```python
import jax
import jax.numpy as jnp
from jax import lax

N = 24576
K = 4


def steps_of(rng, shape, split, smallest, top_value):
    level = 1.0
    for dim, shards_of in split:
        heights = jax.random.uniform(jax.random.fold_in(jax.random.fold_in(rng, 6), dim), (shards_of,), jnp.float32, smallest / len(split), top_value / len(split))
        level = level * jnp.repeat(jnp.exp(heights), shape[dim] // shards_of).reshape((-1,) + (1,) * (len(shape) - 1 - dim))
    return level


def normal_values(key, shape, scale, bound, shards=(), held_as=jnp.bfloat16):
    gain = steps_of(key, shape, shards, -0.22, 0.18) if shards else 1.0
    values = jax.random.normal(key, shape, jnp.float32) * scale * gain
    return jnp.minimum(jnp.maximum(values, -bound), bound).astype(held_as)


def setup_inputs(seed: int = 0) -> dict:
    key_list = jax.random.split(jax.random.key(seed), 2)
    matrix = normal_values(key_list[0], (N, N), 1.0, 6.0, ((0, 8), (1, 32)), jnp.float32)
    return dict(matrix=matrix)


precise = lax.Precision.HIGHEST

def householder(pivot_value, squares):
    length = jnp.sqrt(pivot_value * pivot_value + squares)
    signed = jnp.where(pivot_value >= 0, 1.0, -1.0)
    diagonal = -signed * length
    factor = (diagonal - pivot_value) / diagonal
    return (factor, pivot_value - diagonal)

def finish(product, cross_dots, y_rows, t_block, factor, panel_step):
    new_column = factor * (product - jnp.dot(cross_dots, y_rows, precision=precise))
    t_column = -factor * jnp.dot(t_block, cross_dots, precision=precise)
    slots = jnp.arange(K, dtype=jnp.int32)
    t_column = jnp.where(slots == panel_step, factor, t_column)
    t_block = jnp.where(slots[None, :] == panel_step, t_column[:, None], t_block)
    y_rows = jnp.where(slots[:, None] == panel_step, new_column[None, :], y_rows)
    return (y_rows, t_block)

def reference(matrix):
    extent = matrix.shape[0]
    all_rows = jnp.arange(extent, dtype=jnp.int32)
    slots = jnp.arange(K, dtype=jnp.int32)

    def advance(panel_step, carried):
        y_rows, v_rows, t_block = carried
        column = lax.dynamic_index_in_dim(matrix, panel_step, 1, keepdims=False)
        v_entry = lax.dynamic_index_in_dim(v_rows, panel_step, 1, keepdims=False)
        column = column - jnp.dot(v_entry, y_rows, precision=precise)
        left_dots = jnp.dot(v_rows, column, precision=precise)
        column = column - jnp.dot(jnp.dot(t_block.T, left_dots, precision=precise), v_rows, precision=precise)
        below = all_rows > panel_step + 1
        squares = jnp.sum(jnp.where(below, column * column, 0.0))
        pivot_value = lax.dynamic_index_in_dim(column, panel_step + 1, 0, keepdims=False)
        factor, divisor = householder(pivot_value, squares)
        reflect = jnp.where(below, column / divisor, 0.0) + (all_rows == panel_step + 1).astype(column.dtype)
        product = jnp.dot(matrix, reflect, precision=precise)
        cross_dots = jnp.dot(v_rows, reflect, precision=precise)
        y_rows, t_block = finish(product, cross_dots, y_rows, t_block, factor, panel_step)
        v_rows = jnp.where(slots[:, None] == panel_step, reflect[None, :], v_rows)
        return (y_rows, v_rows, t_block)
    start = (jnp.zeros((K, extent), jnp.float32), jnp.zeros((K, extent), jnp.float32), jnp.zeros((K, K), jnp.float32))
    y_rows, v_rows, t_block = lax.fori_loop(0, K, advance, start)
    return (y_rows, v_rows, t_block)
```

```python
import functools

import jax
import jax.numpy as jnp
from jax import lax
from jax.experimental import pallas as pl
from jax.experimental.pallas import tpu as pltpu
from jax.sharding import Mesh, PartitionSpec as P

K = 4
LANES = 128
NX, NCORE, NZ, NY = 4, 2, 8, 4
GROUP = 16
BLOCK = 24
PAIR = NCORE * BLOCK
FULL = NX * PAIR
SLICE = BLOCK // NZ
PART = PAIR // NY
WIDE = 6
CHUNKS = 8

f32 = jnp.float32
VMEM = pl.BlockSpec(memory_space=pltpu.VMEM)
ANY = pl.BlockSpec(memory_space=pl.ANY)


def params(mib):
    return pltpu.CompilerParams(vmem_limit_bytes=mib << 20)


def vec(*shape):
    return jax.ShapeDtypeStruct(shape, f32)


def total(value):
    return jnp.sum(jnp.sum(value, axis=0, keepdims=True), axis=1, keepdims=True)


def take_panel(a_ref, out_ref, cols):
    for block in range(BLOCK):
        turned = a_ref[block * LANES : (block + 1) * LANES, :].T
        for i in range(K):
            cols[i, block : block + 1, :] = turned[i : i + 1, :]
    first = cols[0]
    for k in range(NCORE):
        for z in range(NZ):
            out_ref[k * NZ + z, :BLOCK, :] = first
            for i in range(1, K):
                at = BLOCK + SLICE * (i - 1)
                out_ref[k * NZ + z, at : at + SLICE, :] = cols[i, SLICE * z : SLICE * (z + 1), :]


def pass_panel(r_ref, out_ref, stage):
    stage[...] = jnp.zeros_like(stage)
    for k in range(NCORE):
        stage[k * BLOCK : (k + 1) * BLOCK, :] = r_ref[k * NZ, :BLOCK, :]
    extra = SLICE * (K - 1)
    own = lax.axis_index("core") * NZ
    stage[PAIR : PAIR + extra, :] = r_ref[own, BLOCK : BLOCK + extra, :]
    for d in range(GROUP):
        out_ref[d] = stage[...]


def pass_product(r_ref, out_ref, stage):
    stage[...] = jnp.zeros_like(stage)
    for k in range(NCORE):
        sums = r_ref[k * NZ, :BLOCK, :]
        for z in range(1, NZ):
            sums = sums + r_ref[k * NZ + z, :BLOCK, :]
        stage[k * BLOCK : (k + 1) * BLOCK, :] = sums
    first = lax.axis_index("y") * NY
    for i in range(NY):
        at = PAIR + SLICE * i
        stage[at : at + SLICE, :] = r_ref[first + i, BLOCK : BLOCK + SLICE, :]
    for d in range(GROUP):
        out_ref[d] = stage[...]


def step(j, *refs):
    if j == 0:
        r_ref, a_ref, v_out, s_out, later_out, x_out, held, vec_ref, sums, sems = refs
    elif j == 1:
        r_ref, later, v_in, s_in, a_ref, v_out, s_out, y_out, x_out, held, vec_ref, sums, sems = refs
    else:
        r_ref, later, v_in, s_in, y_in, a_ref, v_out, s_out, y_out, x_out, held, vec_ref, sums, sems = refs

    rows = held.shape[0] // CHUNKS
    copies = [
        pltpu.make_async_copy(
            a_ref.at[pl.ds(n * rows, rows), :], held.at[pl.ds(n * rows, rows), :], sems.at[n]
        )
        for n in range(CHUNKS)
    ]
    for copy in copies:
        copy.start()

    line = lax.broadcasted_iota(jnp.int32, (8, LANES), 0)
    lane = lax.broadcasted_iota(jnp.int32, (8, LANES), 1)
    index = lax.broadcasted_iota(jnp.int32, (FULL, LANES), 0) * LANES + lax.broadcasted_iota(
        jnp.int32, (FULL, LANES), 1
    )
    if j == 0:
        for x in range(NX):
            vec_ref[x * PAIR : (x + 1) * PAIR, :] = r_ref[x * NY, :PAIR, :]
        extra = SLICE * (K - 1)
        later_out[:extra, :] = r_ref[lax.axis_index("x") * NY, PAIR : PAIR + extra, :]
        column = vec_ref[...]
        state = jnp.zeros((8, LANES), f32)
        vs = []
    else:
        state = s_in[...]
        vs = [v_in[i] for i in range(j)]
        ys = [y_in[i] for i in range(j - 1)] if j > 1 else []
        for x in range(NX):
            sums_x = r_ref[x * NY, :PAIR, :]
            for y in range(1, NY):
                sums_x = sums_x + r_ref[x * NY + y, :PAIR, :]
            vec_ref[x * PAIR : (x + 1) * PAIR, :] = sums_x
        product = vec_ref[...]
        for i in range(j - 1):
            product = product - state[4 + i : 5 + i, j - 1 : j] * ys[i]
        ys.append(state[j - 1 : j, j - 1 : j] * product)
        for i in range(j):
            y_out[i] = ys[i]
        for x in range(NX):
            for y in range(NY):
                at = PAIR * x + PART * y
                vec_ref[at : at + PART, :] = r_ref[x * NY + y, PAIR : PAIR + PART, :]
        column = vec_ref[...]
        for i in range(j):
            column = column - vs[i][0:1, j : j + 1] * ys[i]
        dots = [total(v * column) for v in vs]
        for k in range(j):
            weight = state[0:1, k : k + 1] * dots[0]
            for i in range(1, k + 1):
                weight = weight + state[i : i + 1, k : k + 1] * dots[i]
            column = column - weight * vs[k]

    below = index > j + 1
    squares = total(jnp.where(below, column * column, 0.0))
    pivot = column[0:1, j + 1 : j + 2]
    length = jnp.sqrt(pivot * pivot + squares)
    beta = jnp.where(pivot >= 0, -length, length)
    tau = (beta - pivot) / beta
    reflect = jnp.where(below, column / (pivot - beta), 0.0) + (index == j + 1).astype(f32)
    vec_ref[...] = reflect

    crosses = [total(v * reflect) for v in vs]
    for i in range(j):
        entry = state[i : i + 1, i : i + 1] * crosses[i]
        for k in range(i + 1, j):
            entry = entry + state[i : i + 1, k : k + 1] * crosses[k]
        state = jnp.where((line == i) & (lane == j), -tau * entry, state)
        state = jnp.where((line == 4 + i) & (lane == j), crosses[i], state)
    s_out[...] = jnp.where((line == j) & (lane == j), tau, state)
    for i in range(j):
        v_out[i] = vs[i]
    v_out[j] = reflect

    mine = (lax.axis_index("z") * NY + lax.axis_index("y")) * WIDE
    parts = [vec_ref[pl.ds(mine + n, 1), :] for n in range(WIDE)]
    for block in range(BLOCK):
        if block % (BLOCK // CHUNKS) == 0:
            copies[block // (BLOCK // CHUNKS)].wait()
        rows = slice(block * LANES, (block + 1) * LANES)
        acc = held[rows, :LANES] * parts[0]
        for n in range(1, WIDE):
            acc = acc + held[rows, n * LANES : (n + 1) * LANES] * parts[n]
        sums[block : block + 1, :] = jnp.sum(acc.T, axis=0, keepdims=True)
    product = sums[...]
    if j == K - 1:
        for d in range(NZ * NY):
            x_out[d] = product
    else:
        source = later_out if j == 0 else later
        piece = source[SLICE * j : SLICE * (j + 1), :]
        for d in range(GROUP):
            x_out[d, :BLOCK, :] = product
            x_out[d, BLOCK : BLOCK + SLICE, :] = piece


def finish(r_ref, v_in, s_in, y_in, y_out, v_out, t_out):
    at = (lax.axis_index("x") * NCORE + lax.axis_index("core")) * BLOCK
    at = pl.multiple_of(at, 8)
    state = s_in[...]
    product = r_ref[0]
    for d in range(1, NZ * NY):
        product = product + r_ref[d]
    ys = [y_in[i, pl.ds(at, BLOCK), :] for i in range(K - 1)]
    for i in range(K - 1):
        product = product - state[4 + i : 5 + i, K - 1 : K] * ys[i]
    ys.append(state[K - 1 : K, K - 1 : K] * product)
    for i in range(K):
        v = v_in[i, pl.ds(at, BLOCK), :]
        for n in range(BLOCK):
            y_out[i : i + 1, n * LANES : (n + 1) * LANES] = ys[i][n : n + 1, :]
            v_out[i : i + 1, n * LANES : (n + 1) * LANES] = v[n : n + 1, :]
    t_out[...] = state[0:K, 0:K]


def swap(value, axes):
    return lax.all_to_all(value, axes, 0, 0, tiled=True)


def on_device(matrix):
    rows_dev, cols_dev = matrix.shape
    first = 40
    second = 64

    sent = pl.pallas_call(
        take_panel,
        grid=(1,),
        in_specs=[pl.BlockSpec((rows_dev, LANES), lambda i: (0, 0))],
        out_specs=pl.BlockSpec((GROUP, first, LANES), lambda i: (0, 0, 0)),
        out_shape=vec(GROUP, first, LANES),
        scratch_shapes=[pltpu.VMEM((K, BLOCK, LANES), f32)],
        compiler_params=params(16),
    )(matrix)
    got = swap(sent, ("core", "z"))
    sent = pl.pallas_call(
        pass_panel,
        in_specs=[VMEM],
        out_specs=VMEM,
        out_shape=vec(GROUP, second, LANES),
        scratch_shapes=[pltpu.VMEM((second, LANES), f32)],
        compiler_params=params(8),
    )(got)
    got = swap(sent, ("x", "y"))

    scratch = [
        pltpu.VMEM((rows_dev, cols_dev), f32),
        pltpu.VMEM((FULL, LANES), f32),
        pltpu.VMEM((BLOCK, LANES), f32),
        pltpu.SemaphoreType.DMA((CHUNKS,)),
    ]
    for j in range(K):
        send = vec(NZ * NY, BLOCK, LANES) if j == K - 1 else vec(GROUP, 32, LANES)
        if j == 0:
            v, s, later, sent = pl.pallas_call(
                functools.partial(step, j),
                in_specs=[VMEM, ANY],
                out_specs=[VMEM] * 4,
                out_shape=[vec(1, FULL, LANES), vec(8, LANES), vec(16, LANES), send],
                scratch_shapes=scratch,
                compiler_params=params(20),
            )(got, matrix)
        else:
            old = [v, s] + ([y] if j > 1 else [])
            v, s, y, sent = pl.pallas_call(
                functools.partial(step, j),
                in_specs=[VMEM] * (2 + len(old)) + [ANY],
                out_specs=[VMEM] * 4,
                out_shape=[vec(j + 1, FULL, LANES), vec(8, LANES), vec(j, FULL, LANES), send],
                scratch_shapes=scratch,
                compiler_params=params(20),
            )(got, later, *old, matrix)
        if j < K - 1:
            got = swap(sent, ("core", "z"))
            sent = pl.pallas_call(
                pass_product,
                in_specs=[VMEM],
                out_specs=VMEM,
                out_shape=vec(GROUP, second, LANES),
                scratch_shapes=[pltpu.VMEM((second, LANES), f32)],
                compiler_params=params(8),
            )(got)
            got = swap(sent, ("x", "y"))
    got = swap(sent, ("z", "y"))
    return pl.pallas_call(
        finish,
        in_specs=[VMEM] * 4,
        out_specs=[VMEM] * 3,
        out_shape=[vec(K, rows_dev), vec(K, rows_dev), vec(K, K)],
        compiler_params=params(8),
    )(got, v, s, y)


def solution(mesh):
    grid = Mesh(mesh.devices.reshape(NX, NCORE, NZ, NY), ("x", "core", "z", "y"))
    return jax.shard_map(
        on_device,
        mesh=grid,
        in_specs=(P(("x", "core"), ("z", "y")),),
        out_specs=(P(None, ("x", "core")), P(None, ("x", "core")), P()),
        check_vma=False,
    )
```

```python
import functools

import jax
import jax.numpy as jnp
from jax import lax
from jax.experimental import pallas as pl
from jax.experimental.pallas import tpu as pltpu
from jax.sharding import Mesh, PartitionSpec as P

K = 4
LANES = 128
NX, NCORE, NZ, NY = 4, 2, 8, 4
GROUP = NX * NY
BLOCK = 24
FULL = NX * NCORE * BLOCK
SLICE = BLOCK // NZ
PART = BLOCK // NY
WIDE = 6

f32 = jnp.float32
VMEM = pl.BlockSpec(memory_space=pltpu.VMEM)


def params(mib):
    return pltpu.CompilerParams(vmem_limit_bytes=mib << 20)


def vec(*shape):
    return jax.ShapeDtypeStruct(shape, f32)


def total(value):
    return jnp.sum(jnp.sum(value, axis=0, keepdims=True), axis=1, keepdims=True)


def take_panel(a_ref, out_ref, cols):
    for block in range(BLOCK):
        turned = a_ref[block * LANES : (block + 1) * LANES, :].T
        for i in range(K):
            cols[i, block : block + 1, :] = turned[i : i + 1, :]
    first = cols[0]
    for z in range(NZ):
        out_ref[z, :BLOCK, :] = first
        for i in range(1, K):
            at = BLOCK + SLICE * (i - 1)
            out_ref[z, at : at + SLICE, :] = cols[i, SLICE * z : SLICE * (z + 1), :]


def pass_panel(r_ref, out_ref):
    for d in range(GROUP):
        out_ref[d] = r_ref[0]


def pick_panel(r_ref, first_ref, later_ref):
    for x in range(NX):
        first_ref[x * BLOCK : (x + 1) * BLOCK, :] = r_ref[x * NY, :BLOCK, :]
    extra = SLICE * (K - 1)
    later_ref[:extra, :] = r_ref[lax.axis_index("x") * NY, BLOCK : BLOCK + extra, :]


def pass_product(r_ref, out_ref, stage):
    sums = r_ref[0, :BLOCK, :]
    for z in range(1, NZ):
        sums = sums + r_ref[z, :BLOCK, :]
    stage[:BLOCK, :] = sums
    first = lax.axis_index("y") * (NZ // NY)
    for i in range(NZ // NY):
        at = BLOCK + SLICE * i
        stage[at : at + SLICE, :] = r_ref[first + i, BLOCK : BLOCK + SLICE, :]
    stage[BLOCK + PART :, :] = jnp.zeros_like(stage[BLOCK + PART :, :])
    for d in range(GROUP):
        out_ref[d] = stage[...]


def pick_product(r_ref, out_ref):
    for x in range(NX):
        sums = r_ref[x * NY, :BLOCK, :]
        for y in range(1, NY):
            sums = sums + r_ref[x * NY + y, :BLOCK, :]
        out_ref[x * BLOCK : (x + 1) * BLOCK, :] = sums
        for y in range(NY):
            at = NX * BLOCK + x * BLOCK + y * PART
            out_ref[at : at + PART, :] = r_ref[x * NY + y, BLOCK : BLOCK + PART, :]


def place(r_ref, offset, vec_ref):
    for x in range(NX):
        for k in range(NCORE):
            at = (x * NCORE + k) * BLOCK
            vec_ref[at : at + BLOCK, :] = r_ref[k, offset + x * BLOCK : offset + (x + 1) * BLOCK, :]
    return vec_ref[...]


def step(j, *refs):
    if j == 0:
        r_ref, later, held, v_out, s_out, x_out, vec_ref, sums = refs
    elif j == 1:
        r_ref, later, v_in, s_in, held, v_out, s_out, y_out, x_out, vec_ref, sums = refs
    else:
        r_ref, later, v_in, s_in, y_in, held, v_out, s_out, y_out, x_out, vec_ref, sums = refs

    line = lax.broadcasted_iota(jnp.int32, (8, LANES), 0)
    lane = lax.broadcasted_iota(jnp.int32, (8, LANES), 1)
    index = lax.broadcasted_iota(jnp.int32, (FULL, LANES), 0) * LANES + lax.broadcasted_iota(
        jnp.int32, (FULL, LANES), 1
    )
    if j == 0:
        column = place(r_ref, 0, vec_ref)
        state = jnp.zeros((8, LANES), f32)
        vs = []
    else:
        state = s_in[...]
        vs = [v_in[i] for i in range(j)]
        ys = [y_in[i] for i in range(j - 1)] if j > 1 else []
        product = place(r_ref, 0, vec_ref)
        for i in range(j - 1):
            product = product - state[4 + i : 5 + i, j - 1 : j] * ys[i]
        ys.append(state[j - 1 : j, j - 1 : j] * product)
        for i in range(j):
            y_out[i] = ys[i]
        column = place(r_ref, NX * BLOCK, vec_ref)
        for i in range(j):
            column = column - vs[i][0:1, j : j + 1] * ys[i]
        dots = [total(v * column) for v in vs]
        for k in range(j):
            weight = state[0:1, k : k + 1] * dots[0]
            for i in range(1, k + 1):
                weight = weight + state[i : i + 1, k : k + 1] * dots[i]
            column = column - weight * vs[k]

    below = index > j + 1
    squares = total(jnp.where(below, column * column, 0.0))
    pivot = column[0:1, j + 1 : j + 2]
    length = jnp.sqrt(pivot * pivot + squares)
    beta = jnp.where(pivot >= 0, -length, length)
    tau = (beta - pivot) / beta
    reflect = jnp.where(below, column / (pivot - beta), 0.0) + (index == j + 1).astype(f32)
    vec_ref[...] = reflect

    crosses = [total(v * reflect) for v in vs]
    for i in range(j):
        entry = state[i : i + 1, i : i + 1] * crosses[i]
        for k in range(i + 1, j):
            entry = entry + state[i : i + 1, k : k + 1] * crosses[k]
        state = jnp.where((line == i) & (lane == j), -tau * entry, state)
        state = jnp.where((line == 4 + i) & (lane == j), crosses[i], state)
    s_out[...] = jnp.where((line == j) & (lane == j), tau, state)
    for i in range(j):
        v_out[i] = vs[i]
    v_out[j] = reflect

    mine = (lax.axis_index("z") * NY + lax.axis_index("y")) * WIDE
    parts = [vec_ref[pl.ds(mine + n, 1), :] for n in range(WIDE)]
    for block in range(BLOCK):
        rows = slice(block * LANES, (block + 1) * LANES)
        acc = held[rows, :LANES] * parts[0]
        for n in range(1, WIDE):
            acc = acc + held[rows, n * LANES : (n + 1) * LANES] * parts[n]
        sums[block : block + 1, :] = jnp.sum(acc.T, axis=0, keepdims=True)
    product = sums[...]
    if j == K - 1:
        for d in range(NZ * NY):
            x_out[d] = product
    else:
        piece = later[SLICE * j : SLICE * (j + 1), :]
        for d in range(NZ):
            x_out[d, :BLOCK, :] = product
            x_out[d, BLOCK : BLOCK + SLICE, :] = piece


def finish(r_ref, v_in, s_in, y_in, y_out, v_out, t_out):
    at = (lax.axis_index("x") * NCORE + lax.axis_index("core")) * BLOCK
    at = pl.multiple_of(at, 8)
    state = s_in[...]
    product = r_ref[0]
    for d in range(1, NZ * NY):
        product = product + r_ref[d]
    ys = [y_in[i, pl.ds(at, BLOCK), :] for i in range(K - 1)]
    for i in range(K - 1):
        product = product - state[4 + i : 5 + i, K - 1 : K] * ys[i]
    ys.append(state[K - 1 : K, K - 1 : K] * product)
    for i in range(K):
        v = v_in[i, pl.ds(at, BLOCK), :]
        for n in range(BLOCK):
            y_out[i : i + 1, n * LANES : (n + 1) * LANES] = ys[i][n : n + 1, :]
            v_out[i : i + 1, n * LANES : (n + 1) * LANES] = v[n : n + 1, :]
    t_out[...] = state[0:K, 0:K]


def swap(value, axes):
    return lax.all_to_all(value, axes, 0, 0, tiled=True)


def on_device(matrix):
    rows_dev, cols_dev = matrix.shape
    first = 40
    second = 32

    sent = pl.pallas_call(
        take_panel,
        in_specs=[VMEM],
        out_specs=VMEM,
        out_shape=vec(NZ, first, LANES),
        scratch_shapes=[pltpu.VMEM((K, BLOCK, LANES), f32)],
        compiler_params=params(8),
    )(matrix[:, :LANES])
    sent = pl.pallas_call(
        pass_panel,
        in_specs=[VMEM],
        out_specs=VMEM,
        out_shape=vec(GROUP, first, LANES),
        compiler_params=params(8),
    )(swap(sent, "z"))
    mine, later = pl.pallas_call(
        pick_panel,
        in_specs=[VMEM],
        out_specs=[VMEM] * 2,
        out_shape=[vec(NX * BLOCK, LANES), vec(16, LANES)],
        compiler_params=params(8),
    )(swap(sent, ("x", "y")))
    got = lax.all_gather(mine, "core")

    scratch = [pltpu.VMEM((FULL, LANES), f32), pltpu.VMEM((BLOCK, LANES), f32)]
    old = []
    for j in range(K):
        send = vec(NZ * NY, BLOCK, LANES) if j == K - 1 else vec(NZ, second, LANES)
        made = [vec(j + 1, FULL, LANES), vec(8, LANES)] + ([vec(j, FULL, LANES)] if j else [])
        *old, sent = pl.pallas_call(
            functools.partial(step, j),
            in_specs=[VMEM] * (3 + len(old)),
            out_specs=[VMEM] * (1 + len(made)),
            out_shape=[*made, send],
            scratch_shapes=scratch,
            compiler_params=params(8),
        )(got, later, *old, matrix)
        if j < K - 1:
            sent = pl.pallas_call(
                pass_product,
                in_specs=[VMEM],
                out_specs=VMEM,
                out_shape=vec(GROUP, second, LANES),
                scratch_shapes=[pltpu.VMEM((second, LANES), f32)],
                compiler_params=params(8),
            )(swap(sent, "z"))
            mine = pl.pallas_call(
                pick_product,
                in_specs=[VMEM],
                out_specs=VMEM,
                out_shape=vec(2 * NX * BLOCK, LANES),
                compiler_params=params(8),
            )(swap(sent, ("x", "y")))
            got = lax.all_gather(mine, "core")
    got = swap(sent, ("z", "y"))
    return pl.pallas_call(
        finish,
        in_specs=[VMEM] * 4,
        out_specs=[VMEM] * 3,
        out_shape=[vec(K, rows_dev), vec(K, rows_dev), vec(K, K)],
        compiler_params=params(8),
    )(got, *old)


def solution(mesh):
    grid = Mesh(mesh.devices.reshape(NX, NCORE, NZ, NY), ("x", "core", "z", "y"))
    return jax.shard_map(
        on_device,
        mesh=grid,
        in_specs=(P(("x", "core"), ("z", "y")),),
        out_specs=(P(None, ("x", "core")), P(None, ("x", "core")), P()),
        check_vma=False,
    )
```

```python
import functools

import jax
import jax.numpy as jnp
from jax import lax
from jax.experimental import pallas as pl
from jax.experimental.pallas import tpu as pltpu
from jax.sharding import Mesh, PartitionSpec as P

K = 4
LANES = 128
NX, NCORE, NZ, NY = 4, 2, 8, 4
GROUP = NX * NY
BLOCK = 24
FULL = NX * NCORE * BLOCK
SLICE = BLOCK // NZ
PART = BLOCK // NY
CHUNKS = 4
WIDE = 6

f32 = jnp.float32
VMEM = pl.BlockSpec(memory_space=pltpu.VMEM)


def params(mib):
    return pltpu.CompilerParams(vmem_limit_bytes=mib << 20)


def vec(*shape):
    return jax.ShapeDtypeStruct(shape, f32)


def total(value):
    return jnp.sum(jnp.sum(value, axis=0, keepdims=True), axis=1, keepdims=True)


def take_panel(a_ref, out_ref, slab, cols, sems):
    @pl.when((lax.axis_index("z") == 0) & (lax.axis_index("y") == 0))
    def _():
        rows = slab.shape[0] // CHUNKS
        copies = []
        for n in range(CHUNKS):
            part = pl.ds(n * rows, rows)
            copies.append(pltpu.make_async_copy(a_ref.at[part, pl.ds(0, LANES)], slab.at[part, :], sems.at[n]))
            copies[n].start()
        for block in range(BLOCK):
            if block % (BLOCK // CHUNKS) == 0:
                copies[block // (BLOCK // CHUNKS)].wait()
            turned = slab[block * LANES : (block + 1) * LANES, :].T
            for i in range(K):
                cols[i, block : block + 1, :] = turned[i : i + 1, :]
        first = cols[0]
        for z in range(NZ):
            out_ref[z, :BLOCK, :] = first
            for i in range(1, K):
                at = BLOCK + SLICE * (i - 1)
                out_ref[z, at : at + SLICE, :] = cols[i, SLICE * z : SLICE * (z + 1), :]


def pass_panel(r_ref, out_ref):
    for d in range(GROUP):
        out_ref[d] = r_ref[0]


def pick_panel(r_ref, first_ref, later_ref):
    for x in range(NX):
        first_ref[x * BLOCK : (x + 1) * BLOCK, :] = r_ref[x * NY, :BLOCK, :]
    extra = SLICE * (K - 1)
    later_ref[:extra, :] = r_ref[lax.axis_index("x") * NY, BLOCK : BLOCK + extra, :]


def pass_product(r_ref, out_ref, stage):
    sums = r_ref[0, :BLOCK, :]
    for z in range(1, NZ):
        sums = sums + r_ref[z, :BLOCK, :]
    stage[:BLOCK, :] = sums
    first = lax.axis_index("y") * (NZ // NY)
    for i in range(NZ // NY):
        at = BLOCK + SLICE * i
        stage[at : at + SLICE, :] = r_ref[first + i, BLOCK : BLOCK + SLICE, :]
    stage[BLOCK + PART :, :] = jnp.zeros_like(stage[BLOCK + PART :, :])
    for d in range(GROUP):
        out_ref[d] = stage[...]


def pick_product(r_ref, out_ref):
    for x in range(NX):
        sums = r_ref[x * NY, :BLOCK, :]
        for y in range(1, NY):
            sums = sums + r_ref[x * NY + y, :BLOCK, :]
        out_ref[x * BLOCK : (x + 1) * BLOCK, :] = sums
        for y in range(NY):
            at = NX * BLOCK + x * BLOCK + y * PART
            out_ref[at : at + PART, :] = r_ref[x * NY + y, BLOCK : BLOCK + PART, :]


def place(r_ref, offset, vec_ref):
    for x in range(NX):
        for k in range(NCORE):
            at = (x * NCORE + k) * BLOCK
            vec_ref[at : at + BLOCK, :] = r_ref[k, offset + x * BLOCK : offset + (x + 1) * BLOCK, :]
    return vec_ref[...]


def step(j, *refs):
    refs = list(refs)
    take = lambda count: [refs.pop(0) for _ in range(count)]
    r_ref, later, held = take(3)
    s_in, v_in, y_in = take(min(j, 1)), take(j), take(max(j - 1, 0))
    v_out, s_out, x_out = take(3)
    y_out = take(min(j, 1))
    vec_ref, sums = take(2)

    line = lax.broadcasted_iota(jnp.int32, (8, LANES), 0)
    lane = lax.broadcasted_iota(jnp.int32, (8, LANES), 1)
    index = lax.broadcasted_iota(jnp.int32, (FULL, LANES), 0) * LANES + lax.broadcasted_iota(
        jnp.int32, (FULL, LANES), 1
    )
    if j == 0:
        column = place(r_ref, 0, vec_ref)
        state = jnp.zeros((8, LANES), f32)
        vs = []
    else:
        state = s_in[0][...]
        vs = [v[...] for v in v_in]
        ys = [y[...] for y in y_in]
        product = place(r_ref, 0, vec_ref)
        for i in range(j - 1):
            product = product - state[4 + i : 5 + i, j - 1 : j] * ys[i]
        ys.append(state[j - 1 : j, j - 1 : j] * product)
        y_out[0][...] = ys[j - 1]
        column = place(r_ref, NX * BLOCK, vec_ref)
        for i in range(j):
            column = column - vs[i][0:1, j : j + 1] * ys[i]
        dots = [total(v * column) for v in vs]
        for k in range(j):
            weight = state[0:1, k : k + 1] * dots[0]
            for i in range(1, k + 1):
                weight = weight + state[i : i + 1, k : k + 1] * dots[i]
            column = column - weight * vs[k]

    below = index > j + 1
    squares = total(jnp.where(below, column * column, 0.0))
    pivot = column[0:1, j + 1 : j + 2]
    length = jnp.sqrt(pivot * pivot + squares)
    beta = jnp.where(pivot >= 0, -length, length)
    tau = (beta - pivot) / beta
    reflect = jnp.where(below, column / (pivot - beta), 0.0) + (index == j + 1).astype(f32)
    vec_ref[...] = reflect

    crosses = [total(v * reflect) for v in vs]
    for i in range(j):
        entry = state[i : i + 1, i : i + 1] * crosses[i]
        for k in range(i + 1, j):
            entry = entry + state[i : i + 1, k : k + 1] * crosses[k]
        state = jnp.where((line == i) & (lane == j), -tau * entry, state)
        state = jnp.where((line == 4 + i) & (lane == j), crosses[i], state)
    s_out[...] = jnp.where((line == j) & (lane == j), tau, state)
    v_out[...] = reflect

    mine = (lax.axis_index("z") * NY + lax.axis_index("y")) * WIDE
    parts = [vec_ref[pl.ds(mine + n, 1), :] for n in range(WIDE)]
    for block in range(BLOCK):
        rows = slice(block * LANES, (block + 1) * LANES)
        acc = held[rows, :LANES] * parts[0]
        for n in range(1, WIDE):
            acc = acc + held[rows, n * LANES : (n + 1) * LANES] * parts[n]
        sums[block : block + 1, :] = jnp.sum(acc.T, axis=0, keepdims=True)
    product = sums[...]
    if j == K - 1:
        for d in range(NZ * NY):
            x_out[d] = product
    else:
        piece = later[SLICE * j : SLICE * (j + 1), :]
        for d in range(NZ):
            x_out[d, :BLOCK, :] = product
            x_out[d, BLOCK : BLOCK + SLICE, :] = piece


def finish(r_ref, s_in, *refs):
    v_in, y_in, (y_out, v_out, t_out) = refs[:K], refs[K : 2 * K - 1], refs[2 * K - 1 :]
    at = (lax.axis_index("x") * NCORE + lax.axis_index("core")) * BLOCK
    at = pl.multiple_of(at, 8)
    state = s_in[...]
    product = r_ref[0]
    for d in range(1, NZ * NY):
        product = product + r_ref[d]
    ys = [y[pl.ds(at, BLOCK), :] for y in y_in]
    for i in range(K - 1):
        product = product - state[4 + i : 5 + i, K - 1 : K] * ys[i]
    ys.append(state[K - 1 : K, K - 1 : K] * product)
    for i in range(K):
        v = v_in[i][pl.ds(at, BLOCK), :]
        for n in range(BLOCK):
            y_out[i : i + 1, n * LANES : (n + 1) * LANES] = ys[i][n : n + 1, :]
            v_out[i : i + 1, n * LANES : (n + 1) * LANES] = v[n : n + 1, :]
    t_out[...] = state[0:K, 0:K]


def swap(value, axes):
    return lax.all_to_all(value, axes, 0, 0, tiled=True)


def on_device(matrix):
    rows_dev, cols_dev = matrix.shape
    first = 40
    second = 32

    sent = pl.pallas_call(
        take_panel,
        in_specs=[pl.BlockSpec(memory_space=pl.ANY)],
        out_specs=VMEM,
        out_shape=vec(NZ, first, LANES),
        scratch_shapes=[
            pltpu.VMEM((rows_dev, LANES), f32),
            pltpu.VMEM((K, BLOCK, LANES), f32),
            pltpu.SemaphoreType.DMA((CHUNKS,)),
        ],
        compiler_params=params(56),
    )(matrix)
    sent = pl.pallas_call(
        pass_panel,
        in_specs=[VMEM],
        out_specs=VMEM,
        out_shape=vec(GROUP, first, LANES),
        cost_estimate=pl.CostEstimate(flops=1 << 32, bytes_accessed=1 << 20, transcendentals=0),
        compiler_params=params(8),
    )(swap(sent, "z"))
    mine, later = pl.pallas_call(
        pick_panel,
        in_specs=[VMEM],
        out_specs=[VMEM] * 2,
        out_shape=[vec(NX * BLOCK, LANES), vec(16, LANES)],
        compiler_params=params(8),
    )(swap(sent, ("x", "y")))
    got = lax.all_gather(mine, "core")

    scratch = [pltpu.VMEM((FULL, LANES), f32), pltpu.VMEM((BLOCK, LANES), f32)]
    state, vs, ys = [], [], []
    for j in range(K):
        send = vec(NZ * NY, BLOCK, LANES) if j == K - 1 else vec(NZ, second, LANES)
        made = [vec(FULL, LANES), vec(8, LANES), send] + [vec(FULL, LANES)] * min(j, 1)
        old = [got, later, matrix, *state, *vs, *ys]
        v, s, sent, *y = pl.pallas_call(
            functools.partial(step, j),
            in_specs=[VMEM] * len(old),
            out_specs=[VMEM] * len(made),
            out_shape=made,
            scratch_shapes=scratch,
            compiler_params=params(8),
        )(*old)
        state, vs, ys = [s], [*vs, v], [*ys, *y]
        if j < K - 1:
            sent = pl.pallas_call(
                pass_product,
                in_specs=[VMEM],
                out_specs=VMEM,
                out_shape=vec(GROUP, second, LANES),
                scratch_shapes=[pltpu.VMEM((second, LANES), f32)],
                compiler_params=params(8),
            )(swap(sent, "z"))
            mine = pl.pallas_call(
                pick_product,
                in_specs=[VMEM],
                out_specs=VMEM,
                out_shape=vec(2 * NX * BLOCK, LANES),
                compiler_params=params(8),
            )(swap(sent, ("x", "y")))
            got = lax.all_gather(mine, "core")
    got = swap(sent, ("z", "y"))
    return pl.pallas_call(
        finish,
        in_specs=[VMEM] * (2 * K + 1),
        out_specs=[VMEM] * 3,
        out_shape=[vec(K, rows_dev), vec(K, rows_dev), vec(K, K)],
        compiler_params=params(8),
    )(got, *state, *vs, *ys)


def solution(mesh):
    grid = Mesh(mesh.devices.reshape(NX, NCORE, NZ, NY), ("x", "core", "z", "y"))
    return jax.shard_map(
        on_device,
        mesh=grid,
        in_specs=(P(("x", "core"), ("z", "y")),),
        out_specs=(P(None, ("x", "core")), P(None, ("x", "core")), P()),
        check_vma=False,
    )
```

```python
import functools

import jax
import jax.numpy as jnp
from jax import lax
from jax.experimental import pallas as pl
from jax.experimental.pallas import tpu as pltpu
from jax.sharding import Mesh, PartitionSpec as P

K = 4
LANES = 128
NX, NCORE, NZ, NY = 4, 2, 8, 4
GROUP = NX * NY
BLOCK = 24
FULL = NX * NCORE * BLOCK
SLICE = BLOCK // NZ
PART = BLOCK // NY
CHUNKS = 4
WIDE = 6

f32 = jnp.float32
VMEM = pl.BlockSpec(memory_space=pltpu.VMEM)


def params(mib):
    return pltpu.CompilerParams(vmem_limit_bytes=mib << 20)


def vec(*shape):
    return jax.ShapeDtypeStruct(shape, f32)


def total(value):
    return jnp.sum(jnp.sum(value, axis=0, keepdims=True), axis=1, keepdims=True)


def take_panel(a_ref, cols_ref, out_ref, slab, sems):
    rows = slab.shape[0] // CHUNKS
    copies = []
    for n in range(CHUNKS):
        part = pl.ds(n * rows, rows)
        copies.append(pltpu.make_async_copy(a_ref.at[part, pl.ds(0, LANES)], slab.at[part, :], sems.at[n]))
        copies[n].start()
    for block in range(BLOCK):
        if block % (BLOCK // CHUNKS) == 0:
            copies[block // (BLOCK // CHUNKS)].wait()
        turned = slab[block * LANES : (block + 1) * LANES, :].T
        for i in range(K):
            cols_ref[i, block : block + 1, :] = turned[i : i + 1, :]
    for d in range(NX * NCORE):
        out_ref[d] = cols_ref[0]


def pack_panel(r_ref, cols_ref, out_ref):
    for z in range(NZ):
        for y in range(NY):
            d = z * NY + y
            out_ref[d, :WIDE, :] = r_ref[z, WIDE * y : WIDE * (y + 1), :]
            for i in range(1, K):
                at = WIDE + SLICE * (i - 1)
                out_ref[d, at : at + SLICE, :] = cols_ref[i, SLICE * z : SLICE * (z + 1), :]


def pick_panel(r_ref, out_ref):
    out_ref[...] = r_ref[0]


def add_over_z(r_ref, stage):
    sums = r_ref[0, :BLOCK, :]
    for z in range(1, NZ):
        sums = sums + r_ref[z, :BLOCK, :]
    stage[:BLOCK, :] = sums


def pass_first(r_ref, out_ref, later_ref, stage):
    add_over_z(r_ref, stage)
    y = lax.axis_index("y") * (NZ // NY)
    for i in range(1, K):
        for n in range(NZ // NY):
            piece = r_ref[y + n, BLOCK + WIDE + SLICE * (i - 1) : BLOCK + WIDE + SLICE * i, :]
            if i == 1:
                stage[BLOCK + SLICE * n : BLOCK + SLICE * (n + 1), :] = piece
            else:
                at = PART * (i - 2) + SLICE * n
                later_ref[at : at + SLICE, :] = piece
    own = lax.axis_index("x") * NCORE + lax.axis_index("core")
    stage[BLOCK + PART : BLOCK + PART + WIDE, :] = r_ref[own, BLOCK : BLOCK + WIDE, :]
    for d in range(GROUP):
        out_ref[d, : BLOCK + PART + WIDE, :] = stage[: BLOCK + PART + WIDE, :]


def pass_product(j, r_ref, later_ref, out_ref, stage):
    add_over_z(r_ref, stage)
    stage[BLOCK : BLOCK + PART, :] = later_ref[PART * (j - 1) : PART * j, :]
    for d in range(GROUP):
        out_ref[d, : BLOCK + PART, :] = stage[: BLOCK + PART, :]


def pick_product(columns, r_ref, out_ref):
    for x in range(NX):
        sums = r_ref[x * NY, :BLOCK, :]
        for y in range(1, NY):
            sums = sums + r_ref[x * NY + y, :BLOCK, :]
        out_ref[x * BLOCK : (x + 1) * BLOCK, :] = sums
        for n in range(columns):
            for y in range(NY):
                at = (1 + n) * NX * BLOCK + x * BLOCK + y * PART
                out_ref[at : at + PART, :] = r_ref[x * NY + y, BLOCK + PART * n : BLOCK + PART * (n + 1), :]


def place(r_ref, offset, vec_ref):
    for x in range(NX):
        for k in range(NCORE):
            at = (x * NCORE + k) * BLOCK
            vec_ref[at : at + BLOCK, :] = r_ref[k, offset + x * BLOCK : offset + (x + 1) * BLOCK, :]
    return vec_ref[...]


def whole_index():
    return lax.broadcasted_iota(jnp.int32, (FULL, LANES), 0) * LANES + lax.broadcasted_iota(
        jnp.int32, (FULL, LANES), 1
    )


def householder(column, j):
    index = whole_index()
    below = index > j + 1
    squares = total(jnp.where(below, column * column, 0.0))
    pivot = column[0:1, j + 1 : j + 2]
    length = jnp.sqrt(pivot * pivot + squares)
    beta = jnp.where(pivot >= 0, -length, length)
    divisor = pivot - beta
    reflect = jnp.where(below, column / divisor, 0.0) + (index == j + 1).astype(f32)
    return reflect, (beta - pivot) / beta, divisor


def multiply(held, parts, sums):
    for block in range(BLOCK):
        rows = slice(block * LANES, (block + 1) * LANES)
        acc = held[rows, :LANES] * parts[0]
        for n in range(1, WIDE):
            acc = acc + held[rows, n * LANES : (n + 1) * LANES] * parts[n]
        sums[block : block + 1, :] = jnp.sum(acc.T, axis=0, keepdims=True)
    return sums[...]


def place_of_columns():
    return (lax.axis_index("z") * NY + lax.axis_index("y")) * WIDE


def first_step(r_ref, held, x_out, sums):
    index = (
        place_of_columns() + lax.broadcasted_iota(jnp.int32, (WIDE, LANES), 0)
    ) * LANES + lax.broadcasted_iota(jnp.int32, (WIDE, LANES), 1)
    below = jnp.where(index > 1, r_ref[:WIDE, :], 0.0)
    product = multiply(held, [below[n : n + 1, :] for n in range(WIDE)], sums)
    extra = WIDE + SLICE * (K - 1)
    for d in range(NZ):
        x_out[d, :BLOCK, :] = product
        x_out[d, BLOCK : BLOCK + extra, :] = r_ref[:extra, :]


def step(j, *refs):
    refs = list(refs)
    take = lambda count: [refs.pop(0) for _ in range(count)]
    r_ref, held = take(2)
    s_in, v_in, y_in = take(j > 1), take(j if j > 1 else 0), take(j - 1)
    v_out, s_out, x_out, y_out = take(4)
    v_first = take(j == 1)
    vec_ref, sums = take(2)

    line = lax.broadcasted_iota(jnp.int32, (8, LANES), 0)
    lane = lax.broadcasted_iota(jnp.int32, (8, LANES), 1)
    vs = [v[...] for v in v_in]
    ys = [y[...] for y in y_in]
    product = place(r_ref, 0, vec_ref)
    column = place(r_ref, NX * BLOCK, vec_ref)
    if j == 1:
        reflect, tau, divisor = householder(place(r_ref, 2 * NX * BLOCK, vec_ref), 0)
        state = jnp.where((line == 0) & (lane == 0), tau, 0.0)
        vs.append(reflect)
        v_first[0][...] = reflect
        product = product / divisor + column
    else:
        state = s_in[0][...]
        for i in range(j - 1):
            product = product - state[4 + i : 5 + i, j - 1 : j] * ys[i]
    ys.append(state[j - 1 : j, j - 1 : j] * product)
    y_out[...] = ys[j - 1]
    for i in range(j):
        column = column - vs[i][0:1, j : j + 1] * ys[i]
    dots = [total(v * column) for v in vs]
    for k in range(j):
        weight = state[0:1, k : k + 1] * dots[0]
        for i in range(1, k + 1):
            weight = weight + state[i : i + 1, k : k + 1] * dots[i]
        column = column - weight * vs[k]
    reflect, tau, _ = householder(column, j)
    vec_ref[...] = reflect
    v_out[...] = reflect

    crosses = [total(v * reflect) for v in vs]
    old = state
    for i in range(j):
        entry = old[i : i + 1, i : i + 1] * crosses[i]
        for k in range(i + 1, j):
            entry = entry + old[i : i + 1, k : k + 1] * crosses[k]
        state = jnp.where((line == i) & (lane == j), -tau * entry, state)
        state = jnp.where((line == 4 + i) & (lane == j), crosses[i], state)
    s_out[...] = jnp.where((line == j) & (lane == j), tau, state)

    mine = place_of_columns()
    product = multiply(held, [vec_ref[pl.ds(mine + n, 1), :] for n in range(WIDE)], sums)
    for d in range(NZ * NY if j == K - 1 else NZ):
        x_out[d] = product


def finish(r_ref, s_in, *refs):
    v_in, y_in, (y_out, v_out, t_out) = refs[:K], refs[K : 2 * K - 1], refs[2 * K - 1 :]
    at = (lax.axis_index("x") * NCORE + lax.axis_index("core")) * BLOCK
    at = pl.multiple_of(at, 8)
    state = s_in[...]
    product = r_ref[0]
    for d in range(1, NZ * NY):
        product = product + r_ref[d]
    ys = [y[pl.ds(at, BLOCK), :] for y in y_in]
    for i in range(K - 1):
        product = product - state[4 + i : 5 + i, K - 1 : K] * ys[i]
    ys.append(state[K - 1 : K, K - 1 : K] * product)
    for i in range(K):
        v = v_in[i][pl.ds(at, BLOCK), :]
        for n in range(BLOCK):
            y_out[i : i + 1, n * LANES : (n + 1) * LANES] = ys[i][n : n + 1, :]
            v_out[i : i + 1, n * LANES : (n + 1) * LANES] = v[n : n + 1, :]
    t_out[...] = state[0:K, 0:K]


def swap(value, axes):
    return lax.all_to_all(value, axes, 0, 0, tiled=True)


def call(kernel, ins, outs, scratch=(), mib=8, **more):
    return pl.pallas_call(
        kernel,
        in_specs=[VMEM] * len(ins),
        out_specs=[VMEM] * len(outs),
        out_shape=[vec(*shape) for shape in outs],
        scratch_shapes=[pltpu.VMEM(shape, f32) for shape in scratch],
        compiler_params=params(mib),
        **more,
    )(*ins)


def spread_panel(matrix):
    cols, sent = pl.pallas_call(
        take_panel,
        in_specs=[pl.BlockSpec(memory_space=pl.ANY)],
        out_specs=[VMEM] * 2,
        out_shape=[vec(K, BLOCK, LANES), vec(NX * NCORE, BLOCK, LANES)],
        scratch_shapes=[pltpu.VMEM((matrix.shape[0], LANES), f32), pltpu.SemaphoreType.DMA((CHUNKS,))],
        compiler_params=params(56),
    )(matrix)
    return call(pack_panel, [swap(sent, ("x", "core")), cols], [(NZ * NY, 16, LANES)])[0]


def on_device(matrix):
    rows_dev, cols_dev = matrix.shape
    wide = BLOCK + 16

    sent = lax.cond(
        (lax.axis_index("z") == 0) & (lax.axis_index("y") == 0),
        spread_panel,
        lambda _: jnp.zeros((NZ * NY, 16, LANES), f32),
        matrix,
    )
    (mine,) = call(
        pick_panel,
        [swap(sent, ("z", "y"))],
        [(16, LANES)],
        cost_estimate=pl.CostEstimate(flops=1 << 32, bytes_accessed=1 << 20, transcendentals=0),
    )
    (sent,) = call(first_step, [mine, matrix], [(NZ, wide, LANES)], [(BLOCK, LANES)])
    sent, later = call(
        pass_first, [swap(sent, "z")], [(GROUP, wide, LANES), (16, LANES)], [(wide, LANES)]
    )
    (mine,) = call(
        functools.partial(pick_product, 2), [swap(sent, ("x", "y"))], [(3 * NX * BLOCK, LANES)]
    )
    state, vs, ys = [], [], []
    for j in range(1, K):
        got = lax.all_gather(mine, "core")
        send = (NZ * NY if j == K - 1 else NZ, BLOCK, LANES)
        whole = (FULL, LANES)
        v, s, sent, y, *first = call(
            functools.partial(step, j),
            [got, matrix, *state, *vs, *ys],
            [whole, (8, LANES), send, whole] + [whole] * (j == 1),
            [whole, (BLOCK, LANES)],
        )
        state, vs, ys = [s], [*first, *vs, v], [*ys, y]
        if j < K - 1:
            (sent,) = call(
                functools.partial(pass_product, j),
                [swap(sent, "z"), later],
                [(GROUP, 32, LANES)],
                [(32, LANES)],
            )
            (mine,) = call(
                functools.partial(pick_product, 1), [swap(sent, ("x", "y"))], [(2 * NX * BLOCK, LANES)]
            )
    got = swap(sent, ("z", "y"))
    return call(finish, [got, *state, *vs, *ys], [(K, rows_dev), (K, rows_dev), (K, K)])


def solution(mesh):
    grid = Mesh(mesh.devices.reshape(NX, NCORE, NZ, NY), ("x", "core", "z", "y"))
    return jax.shard_map(
        on_device,
        mesh=grid,
        in_specs=(P(("x", "core"), ("z", "y")),),
        out_specs=(P(None, ("x", "core")), P(None, ("x", "core")), P()),
        check_vma=False,
    )
```

```python
import functools

import jax
import jax.numpy as jnp
from jax import lax
from jax.experimental import pallas as pl
from jax.experimental.pallas import tpu as pltpu
from jax.sharding import Mesh, PartitionSpec as P

K = 4
LANES = 128
NX, NCORE, NZ, NY = 4, 2, 8, 4
GROUP = NX * NY
BLOCK = 24
FULL = NX * NCORE * BLOCK
SLICE = BLOCK // NZ
PART = BLOCK // NY
CHUNKS = 8
WIDE = 6

f32 = jnp.float32
VMEM = pl.BlockSpec(memory_space=pltpu.VMEM)


def params(mib):
    return pltpu.CompilerParams(vmem_limit_bytes=mib << 20)


def vec(*shape):
    return jax.ShapeDtypeStruct(shape, f32)


def total(value):
    return jnp.sum(jnp.sum(value, axis=0, keepdims=True), axis=1, keepdims=True)


def take_panel(a_ref, cols_ref, out_ref, slab, sems):
    rows = slab.shape[0] // CHUNKS
    copies = []
    for n in range(CHUNKS):
        part = pl.ds(n * rows, rows)
        copies.append(pltpu.make_async_copy(a_ref.at[part, pl.ds(0, LANES)], slab.at[part, :], sems.at[n]))
        copies[n].start()
    for block in range(BLOCK):
        if block % (BLOCK // CHUNKS) == 0:
            copies[block // (BLOCK // CHUNKS)].wait()
        turned = slab[block * LANES : (block + 1) * LANES, :].T
        for i in range(K):
            cols_ref[i, block : block + 1, :] = turned[i : i + 1, :]
    for d in range(NX * NCORE):
        out_ref[d] = cols_ref[0]


def pack_panel(r_ref, cols_ref, out_ref):
    for z in range(NZ):
        for y in range(NY):
            d = z * NY + y
            out_ref[d, :WIDE, :] = r_ref[z, WIDE * y : WIDE * (y + 1), :]
            for i in range(1, K):
                at = WIDE + SLICE * (i - 1)
                out_ref[d, at : at + SLICE, :] = cols_ref[i, SLICE * z : SLICE * (z + 1), :]


def pick_panel(r_ref, out_ref):
    out_ref[...] = r_ref[0]


def add_over_z(r_ref, stage):
    sums = r_ref[0, :BLOCK, :]
    for z in range(1, NZ):
        sums = sums + r_ref[z, :BLOCK, :]
    stage[:BLOCK, :] = sums


def pass_first(r_ref, out_ref, later_ref, stage):
    add_over_z(r_ref, stage)
    y = lax.axis_index("y") * (NZ // NY)
    for i in range(1, K):
        for n in range(NZ // NY):
            piece = r_ref[y + n, BLOCK + WIDE + SLICE * (i - 1) : BLOCK + WIDE + SLICE * i, :]
            if i == 1:
                stage[BLOCK + SLICE * n : BLOCK + SLICE * (n + 1), :] = piece
            else:
                at = PART * (i - 2) + SLICE * n
                later_ref[at : at + SLICE, :] = piece
    own = lax.axis_index("x") * NCORE + lax.axis_index("core")
    stage[BLOCK + PART : BLOCK + PART + WIDE, :] = r_ref[own, BLOCK : BLOCK + WIDE, :]
    for d in range(GROUP):
        out_ref[d, : BLOCK + PART + WIDE, :] = stage[: BLOCK + PART + WIDE, :]


def pass_product(j, r_ref, later_ref, out_ref, stage):
    add_over_z(r_ref, stage)
    stage[BLOCK : BLOCK + PART, :] = later_ref[PART * (j - 1) : PART * j, :]
    for d in range(GROUP):
        out_ref[d, : BLOCK + PART, :] = stage[: BLOCK + PART, :]


def pick_product(columns, r_ref, out_ref):
    for x in range(NX):
        sums = r_ref[x * NY, :BLOCK, :]
        for y in range(1, NY):
            sums = sums + r_ref[x * NY + y, :BLOCK, :]
        out_ref[x * BLOCK : (x + 1) * BLOCK, :] = sums
        for n in range(columns):
            for y in range(NY):
                at = (1 + n) * NX * BLOCK + x * BLOCK + y * PART
                out_ref[at : at + PART, :] = r_ref[x * NY + y, BLOCK + PART * n : BLOCK + PART * (n + 1), :]


def place(r_ref, offset, vec_ref):
    for x in range(NX):
        for k in range(NCORE):
            at = (x * NCORE + k) * BLOCK
            vec_ref[at : at + BLOCK, :] = r_ref[k, offset + x * BLOCK : offset + (x + 1) * BLOCK, :]
    return vec_ref[...]


def whole_index():
    return lax.broadcasted_iota(jnp.int32, (FULL, LANES), 0) * LANES + lax.broadcasted_iota(
        jnp.int32, (FULL, LANES), 1
    )


def householder(column, j):
    index = whole_index()
    below = index > j + 1
    squares = total(jnp.where(below, column * column, 0.0))
    pivot = column[0:1, j + 1 : j + 2]
    length = jnp.sqrt(pivot * pivot + squares)
    beta = jnp.where(pivot >= 0, -length, length)
    divisor = pivot - beta
    reflect = jnp.where(below, column / divisor, 0.0) + (index == j + 1).astype(f32)
    return reflect, (beta - pivot) / beta, divisor


def multiply(held, parts, sums):
    for block in range(BLOCK):
        rows = slice(block * LANES, (block + 1) * LANES)
        acc = held[rows, :LANES] * parts[0]
        for n in range(1, WIDE):
            acc = acc + held[rows, n * LANES : (n + 1) * LANES] * parts[n]
        sums[block : block + 1, :] = jnp.sum(acc.T, axis=0, keepdims=True)
    return sums[...]


def place_of_columns():
    return (lax.axis_index("z") * NY + lax.axis_index("y")) * WIDE


def first_step(r_ref, held, x_out, sums):
    index = (
        place_of_columns() + lax.broadcasted_iota(jnp.int32, (WIDE, LANES), 0)
    ) * LANES + lax.broadcasted_iota(jnp.int32, (WIDE, LANES), 1)
    below = jnp.where(index > 1, r_ref[:WIDE, :], 0.0)
    product = multiply(held, [below[n : n + 1, :] for n in range(WIDE)], sums)
    extra = WIDE + SLICE * (K - 1)
    for d in range(NZ):
        x_out[d, :BLOCK, :] = product
        x_out[d, BLOCK : BLOCK + extra, :] = r_ref[:extra, :]


def step(j, *refs):
    refs = list(refs)
    take = lambda count: [refs.pop(0) for _ in range(count)]
    r_ref, held = take(2)
    s_in, v_in, y_in = take(j > 1), take(j if j > 1 else 0), take(j - 1)
    v_out, s_out, x_out, y_out = take(4)
    v_first = take(j == 1)
    vec_ref, sums = take(2)

    line = lax.broadcasted_iota(jnp.int32, (8, LANES), 0)
    lane = lax.broadcasted_iota(jnp.int32, (8, LANES), 1)
    vs = [v[...] for v in v_in]
    ys = [y[...] for y in y_in]
    product = place(r_ref, 0, vec_ref)
    column = place(r_ref, NX * BLOCK, vec_ref)
    if j == 1:
        reflect, tau, divisor = householder(place(r_ref, 2 * NX * BLOCK, vec_ref), 0)
        state = jnp.where((line == 0) & (lane == 0), tau, 0.0)
        vs.append(reflect)
        v_first[0][...] = reflect
        product = product / divisor + column
    else:
        state = s_in[0][...]
        for i in range(j - 1):
            product = product - state[4 + i : 5 + i, j - 1 : j] * ys[i]
    ys.append(state[j - 1 : j, j - 1 : j] * product)
    y_out[...] = ys[j - 1]
    for i in range(j):
        column = column - vs[i][0:1, j : j + 1] * ys[i]
    dots = [total(v * column) for v in vs]
    for k in range(j):
        weight = state[0:1, k : k + 1] * dots[0]
        for i in range(1, k + 1):
            weight = weight + state[i : i + 1, k : k + 1] * dots[i]
        column = column - weight * vs[k]
    reflect, tau, _ = householder(column, j)
    vec_ref[...] = reflect
    v_out[...] = reflect

    crosses = [total(v * reflect) for v in vs]
    old = state
    for i in range(j):
        entry = old[i : i + 1, i : i + 1] * crosses[i]
        for k in range(i + 1, j):
            entry = entry + old[i : i + 1, k : k + 1] * crosses[k]
        state = jnp.where((line == i) & (lane == j), -tau * entry, state)
        state = jnp.where((line == 4 + i) & (lane == j), crosses[i], state)
    s_out[...] = jnp.where((line == j) & (lane == j), tau, state)

    mine = place_of_columns()
    product = multiply(held, [vec_ref[pl.ds(mine + n, 1), :] for n in range(WIDE)], sums)
    for d in range(NZ * NY if j == K - 1 else NZ):
        x_out[d] = product


def finish(r_ref, s_in, *refs):
    v_in, y_in, (y_out, v_out, t_out) = refs[:K], refs[K : 2 * K - 1], refs[2 * K - 1 :]
    at = (lax.axis_index("x") * NCORE + lax.axis_index("core")) * BLOCK
    at = pl.multiple_of(at, 8)
    state = s_in[...]
    product = r_ref[0]
    for d in range(1, NZ * NY):
        product = product + r_ref[d]
    ys = [y[pl.ds(at, BLOCK), :] for y in y_in]
    for i in range(K - 1):
        product = product - state[4 + i : 5 + i, K - 1 : K] * ys[i]
    ys.append(state[K - 1 : K, K - 1 : K] * product)
    for i in range(K):
        v = v_in[i][pl.ds(at, BLOCK), :]
        for n in range(BLOCK):
            y_out[i : i + 1, n * LANES : (n + 1) * LANES] = ys[i][n : n + 1, :]
            v_out[i : i + 1, n * LANES : (n + 1) * LANES] = v[n : n + 1, :]
    t_out[...] = state[0:K, 0:K]


def swap(value, axes):
    return lax.all_to_all(value, axes, 0, 0, tiled=True)


def call(kernel, ins, outs, scratch=(), mib=8, **more):
    return pl.pallas_call(
        kernel,
        in_specs=[VMEM] * len(ins),
        out_specs=[VMEM] * len(outs),
        out_shape=[vec(*shape) for shape in outs],
        scratch_shapes=[pltpu.VMEM(shape, f32) for shape in scratch],
        compiler_params=params(mib),
        **more,
    )(*ins)


def spread_panel(matrix):
    cols, sent = pl.pallas_call(
        take_panel,
        in_specs=[pl.BlockSpec(memory_space=pl.ANY)],
        out_specs=[VMEM] * 2,
        out_shape=[vec(K, BLOCK, LANES), vec(NX * NCORE, BLOCK, LANES)],
        scratch_shapes=[pltpu.VMEM((matrix.shape[0], LANES), f32), pltpu.SemaphoreType.DMA((CHUNKS,))],
        compiler_params=params(48),
    )(matrix)
    return call(pack_panel, [swap(sent, ("x", "core")), cols], [(NZ * NY, 16, LANES)])[0]


def on_device(matrix):
    rows_dev, cols_dev = matrix.shape
    wide = BLOCK + 16

    sent = lax.cond(
        (lax.axis_index("z") == 0) & (lax.axis_index("y") == 0),
        spread_panel,
        lambda _: jnp.zeros((NZ * NY, 16, LANES), f32),
        matrix,
    )
    (mine,) = call(
        pick_panel,
        [swap(sent, ("z", "y"))],
        [(16, LANES)],
        cost_estimate=pl.CostEstimate(flops=1 << 32, bytes_accessed=1 << 20, transcendentals=0),
    )
    (sent,) = call(first_step, [mine, matrix], [(NZ, wide, LANES)], [(BLOCK, LANES)])
    sent, later = call(
        pass_first, [swap(sent, "z")], [(GROUP, wide, LANES), (16, LANES)], [(wide, LANES)]
    )
    (mine,) = call(
        functools.partial(pick_product, 2), [swap(sent, ("x", "y"))], [(3 * NX * BLOCK, LANES)]
    )
    state, vs, ys = [], [], []
    for j in range(1, K):
        got = lax.all_gather(mine, "core")
        send = (NZ * NY if j == K - 1 else NZ, BLOCK, LANES)
        whole = (FULL, LANES)
        v, s, sent, y, *first = call(
            functools.partial(step, j),
            [got, matrix, *state, *vs, *ys],
            [whole, (8, LANES), send, whole] + [whole] * (j == 1),
            [whole, (BLOCK, LANES)],
        )
        state, vs, ys = [s], [*first, *vs, v], [*ys, y]
        if j < K - 1:
            (sent,) = call(
                functools.partial(pass_product, j),
                [swap(sent, "z"), later],
                [(GROUP, 32, LANES)],
                [(32, LANES)],
            )
            (mine,) = call(
                functools.partial(pick_product, 1), [swap(sent, ("x", "y"))], [(2 * NX * BLOCK, LANES)]
            )
    got = swap(sent, ("z", "y"))
    return call(finish, [got, *state, *vs, *ys], [(K, rows_dev), (K, rows_dev), (K, K)])


def solution(mesh):
    grid = Mesh(mesh.devices.reshape(NX, NCORE, NZ, NY), ("x", "core", "z", "y"))
    return jax.shard_map(
        on_device,
        mesh=grid,
        in_specs=(P(("x", "core"), ("z", "y")),),
        out_specs=(P(None, ("x", "core")), P(None, ("x", "core")), P()),
        check_vma=False,
    )
```

```python
import functools

import jax
import jax.numpy as jnp
from jax import lax
from jax.experimental import pallas as pl
from jax.experimental.pallas import tpu as pltpu
from jax.sharding import Mesh, PartitionSpec as P

K = 4
LANES = 128
NX, NCORE, NZ, NY = 4, 2, 8, 4
GROUP = NX * NY
BLOCK = 24
FULL = NX * NCORE * BLOCK
SLICE = BLOCK // NZ
SHARE = LANES // NY
CHUNKS = 8
WIDE = 6

f32 = jnp.float32
VMEM = pl.BlockSpec(memory_space=pltpu.VMEM)


def params(mib):
    return pltpu.CompilerParams(vmem_limit_bytes=mib << 20)


def vec(*shape):
    return jax.ShapeDtypeStruct(shape, f32)


def total(value):
    return jnp.sum(jnp.sum(value, axis=0, keepdims=True), axis=1, keepdims=True)


def take_panel(a_ref, cols_ref, out_ref, slab, sems):
    rows = slab.shape[0] // CHUNKS
    copies = []
    for n in range(CHUNKS):
        part = pl.ds(n * rows, rows)
        copies.append(pltpu.make_async_copy(a_ref.at[part, pl.ds(0, LANES)], slab.at[part, :], sems.at[n]))
        copies[n].start()
    for block in range(BLOCK):
        if block % (BLOCK // CHUNKS) == 0:
            copies[block // (BLOCK // CHUNKS)].wait()
        turned = slab[block * LANES : (block + 1) * LANES, :].T
        for i in range(K):
            cols_ref[i, block : block + 1, :] = turned[i : i + 1, :]
    for d in range(NX * NCORE):
        out_ref[d] = cols_ref[0]


def quarter():
    return lax.broadcasted_iota(jnp.int32, (BLOCK, LANES), 1) // SHARE


def pack_panel(r_ref, cols_ref, out_ref, packed):
    for y in range(NY):
        side = cols_ref[0] if y == 0 else pltpu.roll(cols_ref[0], (LANES - SHARE * y) % LANES, 1)
        for i in range(1, K):
            turn = SHARE * (i - y) % LANES
            side = jnp.where(quarter() == i, pltpu.roll(cols_ref[i], turn, 1) if turn else cols_ref[i], side)
        packed[y] = side
    for z in range(NZ):
        for y in range(NY):
            d = z * NY + y
            for n in range(WIDE):
                out_ref[d, :, n * LANES : (n + 1) * LANES] = r_ref[z, WIDE * y + n : WIDE * y + n + 1, :]
            for n in range(SLICE):
                at = (WIDE + n) * LANES
                out_ref[d, :, at : at + LANES] = packed[y, SLICE * z + n : SLICE * z + n + 1, :]


def pick_panel(r_ref, out_ref):
    for n in range(WIDE + SLICE):
        out_ref[n : n + 1, :] = r_ref[0, :, n * LANES : (n + 1) * LANES]


def add_over_z(r_ref, stage):
    sums = r_ref[0, :BLOCK, :]
    for z in range(1, NZ):
        sums = sums + r_ref[z, :BLOCK, :]
    stage[:BLOCK, :] = sums


def pass_first(r_ref, out_ref, stage):
    add_over_z(r_ref, stage)
    for z in range(NZ):
        stage[BLOCK + SLICE * z : BLOCK + SLICE * (z + 1), :] = r_ref[z, BLOCK : BLOCK + SLICE, :]
    for d in range(GROUP):
        out_ref[d] = stage[...]


def pass_product(r_ref, out_ref, stage):
    add_over_z(r_ref, stage)
    for d in range(GROUP):
        out_ref[d] = stage[...]


def add_over_y(r_ref, out_ref):
    for x in range(NX):
        sums = r_ref[x * NY, :BLOCK, :]
        for y in range(1, NY):
            sums = sums + r_ref[x * NY + y, :BLOCK, :]
        out_ref[x * BLOCK : (x + 1) * BLOCK, :] = sums


def pick_first(r_ref, out_ref, later_ref):
    add_over_y(r_ref, out_ref)
    for x in range(NX):
        sides = [r_ref[x * NY + y, BLOCK:, :] for y in range(NY)]
        for i in range(K):
            block = sides[0]
            for y in range(NY):
                turn = SHARE * (y - i) % LANES
                side = pltpu.roll(sides[y], turn, 1) if turn else sides[y]
                block = jnp.where(quarter() == y, side, block)
            if i < 2:
                at = (2 - i) * NX * BLOCK + x * BLOCK
                out_ref[at : at + BLOCK, :] = block
            else:
                at = (i - 2) * NX * BLOCK + x * BLOCK
                later_ref[at : at + BLOCK, :] = block


def pick_product(j, r_ref, later_ref, out_ref):
    add_over_y(r_ref, out_ref)
    out_ref[NX * BLOCK :, :] = later_ref[(j - 1) * NX * BLOCK : j * NX * BLOCK, :]


def place(r_ref, offset, vec_ref):
    for x in range(NX):
        for k in range(NCORE):
            at = (x * NCORE + k) * BLOCK
            vec_ref[at : at + BLOCK, :] = r_ref[k, offset + x * BLOCK : offset + (x + 1) * BLOCK, :]
    return vec_ref[...]


def whole_index():
    return lax.broadcasted_iota(jnp.int32, (FULL, LANES), 0) * LANES + lax.broadcasted_iota(
        jnp.int32, (FULL, LANES), 1
    )


def householder(column, j):
    index = whole_index()
    below = index > j + 1
    squares = total(jnp.where(below, column * column, 0.0))
    pivot = column[0:1, j + 1 : j + 2]
    length = jnp.sqrt(pivot * pivot + squares)
    beta = jnp.where(pivot >= 0, -length, length)
    divisor = pivot - beta
    reflect = jnp.where(below, column / divisor, 0.0) + (index == j + 1).astype(f32)
    return reflect, (beta - pivot) / beta, divisor


def multiply(held, parts, sums):
    for block in range(BLOCK):
        rows = slice(block * LANES, (block + 1) * LANES)
        acc = held[rows, :LANES] * parts[0]
        for n in range(1, WIDE):
            acc = acc + held[rows, n * LANES : (n + 1) * LANES] * parts[n]
        sums[block : block + 1, :] = jnp.sum(acc.T, axis=0, keepdims=True)
    return sums[...]


def place_of_columns():
    return (lax.axis_index("z") * NY + lax.axis_index("y")) * WIDE


def first_step(r_ref, held, x_out, sums):
    index = (
        place_of_columns() + lax.broadcasted_iota(jnp.int32, (WIDE, LANES), 0)
    ) * LANES + lax.broadcasted_iota(jnp.int32, (WIDE, LANES), 1)
    below = jnp.where(index > 1, r_ref[:WIDE, :], 0.0)
    product = multiply(held, [below[n : n + 1, :] for n in range(WIDE)], sums)
    for d in range(NZ):
        x_out[d, :BLOCK, :] = product
        x_out[d, BLOCK : BLOCK + SLICE, :] = r_ref[WIDE : WIDE + SLICE, :]


def step(j, *refs):
    refs = list(refs)
    take = lambda count: [refs.pop(0) for _ in range(count)]
    r_ref, held = take(2)
    s_in, v_in, y_in = take(j > 1), take(j if j > 1 else 0), take(j - 1)
    v_out, s_out, x_out, y_out = take(4)
    v_first = take(j == 1)
    vec_ref, sums = take(2)

    line = lax.broadcasted_iota(jnp.int32, (8, LANES), 0)
    lane = lax.broadcasted_iota(jnp.int32, (8, LANES), 1)
    vs = [v[...] for v in v_in]
    ys = [y[...] for y in y_in]
    product = place(r_ref, 0, vec_ref)
    column = place(r_ref, NX * BLOCK, vec_ref)
    if j == 1:
        reflect, tau, divisor = householder(place(r_ref, 2 * NX * BLOCK, vec_ref), 0)
        state = jnp.where((line == 0) & (lane == 0), tau, 0.0)
        vs.append(reflect)
        v_first[0][...] = reflect
        product = product / divisor + column
    else:
        state = s_in[0][...]
        for i in range(j - 1):
            product = product - state[4 + i : 5 + i, j - 1 : j] * ys[i]
    ys.append(state[j - 1 : j, j - 1 : j] * product)
    y_out[...] = ys[j - 1]
    for i in range(j):
        column = column - vs[i][0:1, j : j + 1] * ys[i]
    dots = [total(v * column) for v in vs]
    for k in range(j):
        weight = state[0:1, k : k + 1] * dots[0]
        for i in range(1, k + 1):
            weight = weight + state[i : i + 1, k : k + 1] * dots[i]
        column = column - weight * vs[k]
    reflect, tau, _ = householder(column, j)
    vec_ref[...] = reflect
    v_out[...] = reflect

    crosses = [total(v * reflect) for v in vs]
    old = state
    for i in range(j):
        entry = old[i : i + 1, i : i + 1] * crosses[i]
        for k in range(i + 1, j):
            entry = entry + old[i : i + 1, k : k + 1] * crosses[k]
        state = jnp.where((line == i) & (lane == j), -tau * entry, state)
        state = jnp.where((line == 4 + i) & (lane == j), crosses[i], state)
    s_out[...] = jnp.where((line == j) & (lane == j), tau, state)

    mine = place_of_columns()
    product = multiply(held, [vec_ref[pl.ds(mine + n, 1), :] for n in range(WIDE)], sums)
    for d in range(NZ * NY if j == K - 1 else NZ):
        x_out[d] = product


def finish(r_ref, s_in, *refs):
    v_in, y_in, (y_out, v_out, t_out) = refs[:K], refs[K : 2 * K - 1], refs[2 * K - 1 :]
    at = (lax.axis_index("x") * NCORE + lax.axis_index("core")) * BLOCK
    at = pl.multiple_of(at, 8)
    state = s_in[...]
    product = r_ref[0]
    for d in range(1, NZ * NY):
        product = product + r_ref[d]
    ys = [y[pl.ds(at, BLOCK), :] for y in y_in]
    for i in range(K - 1):
        product = product - state[4 + i : 5 + i, K - 1 : K] * ys[i]
    ys.append(state[K - 1 : K, K - 1 : K] * product)
    for i in range(K):
        v = v_in[i][pl.ds(at, BLOCK), :]
        for n in range(BLOCK):
            y_out[i : i + 1, n * LANES : (n + 1) * LANES] = ys[i][n : n + 1, :]
            v_out[i : i + 1, n * LANES : (n + 1) * LANES] = v[n : n + 1, :]
    t_out[...] = state[0:K, 0:K]


def swap(value, axes):
    return lax.all_to_all(value, axes, 0, 0, tiled=True)


def call(kernel, ins, outs, scratch=(), mib=8, **more):
    return pl.pallas_call(
        kernel,
        in_specs=[VMEM] * len(ins),
        out_specs=[VMEM] * len(outs),
        out_shape=[vec(*shape) for shape in outs],
        scratch_shapes=[pltpu.VMEM(shape, f32) for shape in scratch],
        compiler_params=params(mib),
        **more,
    )(*ins)


def spread_panel(matrix):
    cols, sent = pl.pallas_call(
        take_panel,
        in_specs=[pl.BlockSpec(memory_space=pl.ANY)],
        out_specs=[VMEM] * 2,
        out_shape=[vec(K, BLOCK, LANES), vec(NX * NCORE, BLOCK, LANES)],
        scratch_shapes=[pltpu.VMEM((matrix.shape[0], LANES), f32), pltpu.SemaphoreType.DMA((CHUNKS,))],
        compiler_params=params(48),
    )(matrix)
    return call(
        pack_panel,
        [swap(sent, ("x", "core")), cols],
        [(NZ * NY, 1, (WIDE + SLICE) * LANES)],
        [(NY, BLOCK, LANES)],
    )[0]


def on_device(matrix):
    rows_dev, cols_dev = matrix.shape

    sent = lax.cond(
        (lax.axis_index("z") == 0) & (lax.axis_index("y") == 0),
        spread_panel,
        lambda _: jnp.zeros((NZ * NY, 1, (WIDE + SLICE) * LANES), f32),
        matrix,
    )
    (mine,) = call(
        pick_panel,
        [swap(sent, ("z", "y"))],
        [(16, LANES)],
        cost_estimate=pl.CostEstimate(flops=1 << 32, bytes_accessed=1 << 20, transcendentals=0),
    )
    (sent,) = call(first_step, [mine, matrix], [(NZ, 32, LANES)], [(BLOCK, LANES)])
    (sent,) = call(pass_first, [swap(sent, "z")], [(GROUP, 2 * BLOCK, LANES)], [(2 * BLOCK, LANES)])
    mine, later = call(
        pick_first, [swap(sent, ("x", "y"))], [(3 * NX * BLOCK, LANES), (2 * NX * BLOCK, LANES)]
    )
    state, vs, ys = [], [], []
    for j in range(1, K):
        got = lax.all_gather(mine, "core")
        send = (NZ * NY if j == K - 1 else NZ, BLOCK, LANES)
        whole = (FULL, LANES)
        v, s, sent, y, *first = call(
            functools.partial(step, j),
            [got, matrix, *state, *vs, *ys],
            [whole, (8, LANES), send, whole] + [whole] * (j == 1),
            [whole, (BLOCK, LANES)],
        )
        state, vs, ys = [s], [*first, *vs, v], [*ys, y]
        if j < K - 1:
            (sent,) = call(pass_product, [swap(sent, "z")], [(GROUP, BLOCK, LANES)], [(BLOCK, LANES)])
            (mine,) = call(
                functools.partial(pick_product, j),
                [swap(sent, ("x", "y")), later],
                [(2 * NX * BLOCK, LANES)],
            )
    got = swap(sent, ("z", "y"))
    return call(finish, [got, *state, *vs, *ys], [(K, rows_dev), (K, rows_dev), (K, K)])


def solution(mesh):
    grid = Mesh(mesh.devices.reshape(NX, NCORE, NZ, NY), ("x", "core", "z", "y"))
    return jax.shard_map(
        on_device,
        mesh=grid,
        in_specs=(P(("x", "core"), ("z", "y")),),
        out_specs=(P(None, ("x", "core")), P(None, ("x", "core")), P()),
        check_vma=False,
    )
```

```python
import functools

import jax
import jax.numpy as jnp
from jax import lax
from jax.experimental import pallas as pl
from jax.experimental.pallas import tpu as pltpu
from jax.sharding import Mesh, PartitionSpec as P

K = 4
LANES = 128
NX, NCORE, NZ, NY = 4, 2, 8, 4
GROUP = NX * NY
BLOCK = 24
FULL = NX * NCORE * BLOCK
SLICE = BLOCK // NZ
SHARE = LANES // NY
CHUNKS = 8
WIDE = 6

f32 = jnp.float32
VMEM = pl.BlockSpec(memory_space=pltpu.VMEM)


def params(mib):
    return pltpu.CompilerParams(vmem_limit_bytes=mib << 20)


def vec(*shape):
    return jax.ShapeDtypeStruct(shape, f32)


def total(value):
    return jnp.sum(jnp.sum(value, axis=0, keepdims=True), axis=1, keepdims=True)


def take_panel(a_ref, cols_ref, out_ref, slab, sems):
    rows = slab.shape[0] // CHUNKS
    copies = []
    for n in range(CHUNKS):
        part = pl.ds(n * rows, rows)
        copies.append(pltpu.make_async_copy(a_ref.at[part, pl.ds(0, LANES)], slab.at[part, :], sems.at[n]))
        copies[n].start()
    for block in range(BLOCK):
        if block % (BLOCK // CHUNKS) == 0:
            copies[block // (BLOCK // CHUNKS)].wait()
        turned = slab[block * LANES : (block + 1) * LANES, :].T
        for i in range(K):
            cols_ref[i, block : block + 1, :] = turned[i : i + 1, :]
    for d in range(NX * NCORE):
        out_ref[d] = cols_ref[0]


def quarter():
    return lax.broadcasted_iota(jnp.int32, (BLOCK, LANES), 1) // SHARE


def pack_panel(r_ref, cols_ref, out_ref, packed):
    for y in range(NY):
        side = cols_ref[0] if y == 0 else pltpu.roll(cols_ref[0], (LANES - SHARE * y) % LANES, 1)
        for i in range(1, K):
            turn = SHARE * (i - y) % LANES
            side = jnp.where(quarter() == i, pltpu.roll(cols_ref[i], turn, 1) if turn else cols_ref[i], side)
        packed[y] = side
    for z in range(NZ):
        for y in range(NY):
            d = z * NY + y
            for n in range(WIDE):
                out_ref[d, :, n * LANES : (n + 1) * LANES] = r_ref[z, WIDE * y + n : WIDE * y + n + 1, :]
            for n in range(SLICE):
                at = (WIDE + n) * LANES
                out_ref[d, :, at : at + LANES] = packed[y, SLICE * z + n : SLICE * z + n + 1, :]


def pick_panel(r_ref, out_ref):
    for n in range(WIDE + SLICE):
        out_ref[n : n + 1, :] = r_ref[0, :, n * LANES : (n + 1) * LANES]


def add_over_z(r_ref, stage):
    sums = r_ref[0, :BLOCK, :]
    for z in range(1, NZ):
        sums = sums + r_ref[z, :BLOCK, :]
    stage[:BLOCK, :] = sums


def pass_first(r_ref, out_ref, stage):
    add_over_z(r_ref, stage)
    for z in range(NZ):
        stage[BLOCK + SLICE * z : BLOCK + SLICE * (z + 1), :] = r_ref[z, BLOCK : BLOCK + SLICE, :]
    for d in range(GROUP):
        out_ref[d] = stage[...]


def pass_product(r_ref, out_ref, stage):
    add_over_z(r_ref, stage)
    for d in range(GROUP):
        out_ref[d] = stage[...]


def add_over_y(r_ref, out_ref):
    for x in range(NX):
        sums = r_ref[x * NY, :BLOCK, :]
        for y in range(1, NY):
            sums = sums + r_ref[x * NY + y, :BLOCK, :]
        out_ref[x * BLOCK : (x + 1) * BLOCK, :] = sums


def pick_first(r_ref, out_ref, later_ref):
    add_over_y(r_ref, out_ref)
    for x in range(NX):
        sides = [r_ref[x * NY + y, BLOCK:, :] for y in range(NY)]
        for i in range(K):
            block = sides[0]
            for y in range(NY):
                turn = SHARE * (y - i) % LANES
                side = pltpu.roll(sides[y], turn, 1) if turn else sides[y]
                block = jnp.where(quarter() == y, side, block)
            if i < 2:
                at = (2 - i) * NX * BLOCK + x * BLOCK
                out_ref[at : at + BLOCK, :] = block
            else:
                at = (i - 2) * NX * BLOCK + x * BLOCK
                later_ref[at : at + BLOCK, :] = block


def pick_product(j, r_ref, later_ref, out_ref):
    add_over_y(r_ref, out_ref)
    out_ref[NX * BLOCK :, :] = later_ref[(j - 1) * NX * BLOCK : j * NX * BLOCK, :]


def far(x):
    return x // (NX // 2)


def place(r_ref, offset, vec_ref):
    side = far(lax.axis_index("x"))
    for x in range(NX):
        for k in range(NCORE):
            at = (x * NCORE + k) * BLOCK
            vec_ref[at : at + BLOCK, :] = r_ref[(side + far(x) + k) % NCORE, offset + x * BLOCK : offset + (x + 1) * BLOCK, :]
    return vec_ref[...]


def whole_index():
    return lax.broadcasted_iota(jnp.int32, (FULL, LANES), 0) * LANES + lax.broadcasted_iota(
        jnp.int32, (FULL, LANES), 1
    )


def householder(column, j):
    index = whole_index()
    below = index > j + 1
    squares = total(jnp.where(below, column * column, 0.0))
    pivot = column[0:1, j + 1 : j + 2]
    length = jnp.sqrt(pivot * pivot + squares)
    beta = jnp.where(pivot >= 0, -length, length)
    divisor = pivot - beta
    reflect = jnp.where(below, column / divisor, 0.0) + (index == j + 1).astype(f32)
    return reflect, (beta - pivot) / beta, divisor, jnp.where(below, column, 0.0)


def multiply(held, parts, sums):
    for block in range(BLOCK):
        rows = slice(block * LANES, (block + 1) * LANES)
        acc = held[rows, :LANES] * parts[0]
        for n in range(1, WIDE):
            acc = acc + held[rows, n * LANES : (n + 1) * LANES] * parts[n]
        sums[block : block + 1, :] = jnp.sum(acc.T, axis=0, keepdims=True)
    return sums[...]


def place_of_columns():
    return (lax.axis_index("z") * NY + lax.axis_index("y")) * WIDE


def first_step(r_ref, held, x_out, sums):
    index = (
        place_of_columns() + lax.broadcasted_iota(jnp.int32, (WIDE, LANES), 0)
    ) * LANES + lax.broadcasted_iota(jnp.int32, (WIDE, LANES), 1)
    below = jnp.where(index > 1, r_ref[:WIDE, :], 0.0)
    product = multiply(held, [below[n : n + 1, :] for n in range(WIDE)], sums)
    for d in range(NZ):
        x_out[d, :BLOCK, :] = product
        x_out[d, BLOCK : BLOCK + SLICE, :] = r_ref[WIDE : WIDE + SLICE, :]


def step(j, *refs):
    refs = list(refs)
    take = lambda count: [refs.pop(0) for _ in range(count)]
    r_ref, held = take(2)
    s_in, v_in, y_in = take(j > 1), take(j if j > 1 else 0), take(j - 1)
    v_out, s_out, x_out, y_out = take(4)
    v_first = take(j == 1)
    vec_ref, sums = take(2)

    line = lax.broadcasted_iota(jnp.int32, (8, LANES), 0)
    lane = lax.broadcasted_iota(jnp.int32, (8, LANES), 1)
    vs = [v[...] for v in v_in]
    ys = [y[...] for y in y_in]
    product = place(r_ref, 0, vec_ref)
    column = place(r_ref, NX * BLOCK, vec_ref)
    if j == 1:
        reflect, tau, divisor, _ = householder(place(r_ref, 2 * NX * BLOCK, vec_ref), 0)
        state = jnp.where((line == 0) & (lane == 0), tau, 0.0)
        vs.append(reflect)
        v_first[0][...] = reflect
    else:
        state = s_in[0][...]
        divisor = state[7:8, j - 1 : j]
    product = product / divisor + column
    if j > 1:
        for i in range(j - 1):
            product = product - state[4 + i : 5 + i, j - 1 : j] * ys[i]
    ys.append(state[j - 1 : j, j - 1 : j] * product)
    y_out[...] = ys[j - 1]
    for i in range(j):
        column = column - vs[i][0:1, j : j + 1] * ys[i]
    dots = [total(v * column) for v in vs]
    for k in range(j):
        weight = state[0:1, k : k + 1] * dots[0]
        for i in range(1, k + 1):
            weight = weight + state[i : i + 1, k : k + 1] * dots[i]
        column = column - weight * vs[k]
    reflect, tau, divisor, undivided = householder(column, j)
    vec_ref[...] = reflect if j == K - 1 else undivided
    v_out[...] = reflect

    crosses = [total(v * reflect) for v in vs]
    old = state
    for i in range(j):
        entry = old[i : i + 1, i : i + 1] * crosses[i]
        for k in range(i + 1, j):
            entry = entry + old[i : i + 1, k : k + 1] * crosses[k]
        state = jnp.where((line == i) & (lane == j), -tau * entry, state)
        state = jnp.where((line == 4 + i) & (lane == j), crosses[i], state)
    state = jnp.where((line == 7) & (lane == j), divisor, state)
    s_out[...] = jnp.where((line == j) & (lane == j), tau, state)

    mine = place_of_columns()
    product = multiply(held, [vec_ref[pl.ds(mine + n, 1), :] for n in range(WIDE)], sums)
    for d in range(NZ * NY if j == K - 1 else NZ):
        x_out[d] = product


def finish(r_ref, s_in, *refs):
    v_in, y_in, (y_out, v_out, t_out) = refs[:K], refs[K : 2 * K - 1], refs[2 * K - 1 :]
    at = (lax.axis_index("x") * NCORE + lax.axis_index("core")) * BLOCK
    at = pl.multiple_of(at, 8)
    state = s_in[...]
    product = r_ref[0]
    for d in range(1, NZ * NY):
        product = product + r_ref[d]
    ys = [y[pl.ds(at, BLOCK), :] for y in y_in]
    for i in range(K - 1):
        product = product - state[4 + i : 5 + i, K - 1 : K] * ys[i]
    ys.append(state[K - 1 : K, K - 1 : K] * product)
    for i in range(K):
        v = v_in[i][pl.ds(at, BLOCK), :]
        for n in range(BLOCK):
            y_out[i : i + 1, n * LANES : (n + 1) * LANES] = ys[i][n : n + 1, :]
            v_out[i : i + 1, n * LANES : (n + 1) * LANES] = v[n : n + 1, :]
    t_out[...] = state[0:K, 0:K]


def swap(value, axes):
    return lax.all_to_all(value, axes, 0, 0, tiled=True)


def swap_across(value):
    place_of = lambda x, k, z, y: ((x * NCORE + k) * NZ + z) * NY + y
    groups = [
        [place_of(x, (k + far(x)) % NCORE, z, y) for x in range(NX) for y in range(NY)]
        for k in range(NCORE)
        for z in range(NZ)
    ]
    return lax.all_to_all(value, ("x", "core", "z", "y"), 0, 0, axis_index_groups=groups, tiled=True)


def call(kernel, ins, outs, scratch=(), mib=8, **more):
    return pl.pallas_call(
        kernel,
        in_specs=[VMEM] * len(ins),
        out_specs=[VMEM] * len(outs),
        out_shape=[vec(*shape) for shape in outs],
        scratch_shapes=[pltpu.VMEM(shape, f32) for shape in scratch],
        compiler_params=params(mib),
        **more,
    )(*ins)


def spread_panel(matrix):
    cols, sent = pl.pallas_call(
        take_panel,
        in_specs=[pl.BlockSpec(memory_space=pl.ANY)],
        out_specs=[VMEM] * 2,
        out_shape=[vec(K, BLOCK, LANES), vec(NX * NCORE, BLOCK, LANES)],
        scratch_shapes=[pltpu.VMEM((matrix.shape[0], LANES), f32), pltpu.SemaphoreType.DMA((CHUNKS,))],
        compiler_params=params(48),
    )(matrix)
    return call(
        pack_panel,
        [swap(sent, ("x", "core")), cols],
        [(NZ * NY, 1, (WIDE + SLICE) * LANES)],
        [(NY, BLOCK, LANES)],
    )[0]


def on_device(matrix):
    rows_dev, cols_dev = matrix.shape

    sent = lax.cond(
        (lax.axis_index("z") == 0) & (lax.axis_index("y") == 0),
        spread_panel,
        lambda _: jnp.zeros((NZ * NY, 1, (WIDE + SLICE) * LANES), f32),
        matrix,
    )
    (mine,) = call(
        pick_panel,
        [swap(sent, ("z", "y"))],
        [(16, LANES)],
        cost_estimate=pl.CostEstimate(flops=1 << 32, bytes_accessed=1 << 20, transcendentals=0),
    )
    (sent,) = call(first_step, [mine, matrix], [(NZ, 32, LANES)], [(BLOCK, LANES)])
    (sent,) = call(pass_first, [swap(sent, "z")], [(GROUP, 2 * BLOCK, LANES)], [(2 * BLOCK, LANES)])
    mine, later = call(
        pick_first, [swap_across(sent)], [(3 * NX * BLOCK, LANES), (2 * NX * BLOCK, LANES)]
    )
    state, vs, ys = [], [], []
    for j in range(1, K):
        got = lax.all_gather(mine, "core")
        send = (NZ * NY if j == K - 1 else NZ, BLOCK, LANES)
        whole = (FULL, LANES)
        v, s, sent, y, *first = call(
            functools.partial(step, j),
            [got, matrix, *state, *vs, *ys],
            [whole, (8, LANES), send, whole] + [whole] * (j == 1),
            [whole, (BLOCK, LANES)],
        )
        state, vs, ys = [s], [*first, *vs, v], [*ys, y]
        if j < K - 1:
            (sent,) = call(pass_product, [swap(sent, "z")], [(GROUP, BLOCK, LANES)], [(BLOCK, LANES)])
            (mine,) = call(
                functools.partial(pick_product, j),
                [swap_across(sent), later],
                [(2 * NX * BLOCK, LANES)],
            )
    got = swap(sent, ("z", "y"))
    return call(finish, [got, *state, *vs, *ys], [(K, rows_dev), (K, rows_dev), (K, K)])


def solution(mesh):
    grid = Mesh(mesh.devices.reshape(NX, NCORE, NZ, NY), ("x", "core", "z", "y"))
    return jax.shard_map(
        on_device,
        mesh=grid,
        in_specs=(P(("x", "core"), ("z", "y")),),
        out_specs=(P(None, ("x", "core")), P(None, ("x", "core")), P()),
        check_vma=False,
    )
```

```python
import functools

import jax
import jax.numpy as jnp
from jax import lax
from jax.experimental import pallas as pl
from jax.experimental.pallas import tpu as pltpu
from jax.sharding import Mesh, PartitionSpec as P

K = 4
LANES = 128
NX, NCORE, NZ, NY = 4, 2, 8, 4
GROUP = NX * NY
BLOCK = 24
FULL = NX * NCORE * BLOCK
SLICE = BLOCK // NZ
CHUNKS = 8
WIDE = 6

f32 = jnp.float32
VMEM = pl.BlockSpec(memory_space=pltpu.VMEM)


def params(mib):
    return pltpu.CompilerParams(vmem_limit_bytes=mib << 20)


def vec(*shape):
    return jax.ShapeDtypeStruct(shape, f32)


def total(value):
    return jnp.sum(jnp.sum(value, axis=0, keepdims=True), axis=1, keepdims=True)


def take_panel(a_ref, cols_ref, out_ref, slab, sems):
    rows = slab.shape[0] // CHUNKS
    copies = []
    for n in range(CHUNKS):
        part = pl.ds(n * rows, rows)
        copies.append(pltpu.make_async_copy(a_ref.at[part, pl.ds(0, LANES)], slab.at[part, :], sems.at[n]))
        copies[n].start()
    for block in range(BLOCK):
        if block % (BLOCK // CHUNKS) == 0:
            copies[block // (BLOCK // CHUNKS)].wait()
        turned = slab[block * LANES : (block + 1) * LANES, :].T
        for i in range(K):
            cols_ref[i, block : block + 1, :] = turned[i : i + 1, :]
    for d in range(NX * NCORE):
        out_ref[d] = cols_ref[0]


def pack_panel(r_ref, cols_ref, out_ref):
    for z in range(NZ):
        for y in range(NY):
            d = z * NY + y
            for n in range(WIDE):
                out_ref[d, :, n * LANES : (n + 1) * LANES] = r_ref[z, WIDE * y + n : WIDE * y + n + 1, :]
            for n in range(SLICE):
                at = (WIDE + n) * LANES
                out_ref[d, :, at : at + LANES] = cols_ref[y, SLICE * z + n : SLICE * z + n + 1, :]


def pick_panel(r_ref, out_ref):
    for n in range(WIDE + SLICE):
        out_ref[n : n + 1, :] = r_ref[0, :, n * LANES : (n + 1) * LANES]


def add_over_z(r_ref, stage):
    sums = r_ref[0, :BLOCK, :]
    for z in range(1, NZ):
        sums = sums + r_ref[z, :BLOCK, :]
    stage[:BLOCK, :] = sums


def pass_first(r_ref, out_ref, stage):
    add_over_z(r_ref, stage)
    for z in range(NZ):
        stage[BLOCK + SLICE * z : BLOCK + SLICE * (z + 1), :] = r_ref[z, BLOCK : BLOCK + SLICE, :]
    for d in range(GROUP):
        out_ref[d] = stage[...]


def pass_product(r_ref, out_ref, stage):
    add_over_z(r_ref, stage)
    for d in range(GROUP):
        out_ref[d] = stage[...]


def add_over_y(r_ref, out_ref):
    for x in range(NX):
        sums = r_ref[x * NY, :BLOCK, :]
        for y in range(1, NY):
            sums = sums + r_ref[x * NY + y, :BLOCK, :]
        out_ref[x * BLOCK : (x + 1) * BLOCK, :] = sums


def pick_first(r_ref, out_ref, later_ref):
    add_over_y(r_ref, out_ref)
    for x in range(NX):
        for y in range(NY):
            block = r_ref[x * NY + y, BLOCK:, :]
            if y < 2:
                at = (2 - y) * NX * BLOCK + x * BLOCK
                out_ref[at : at + BLOCK, :] = block
            else:
                at = (y - 2) * NX * BLOCK + x * BLOCK
                later_ref[at : at + BLOCK, :] = block


def pick_product(j, r_ref, later_ref, out_ref):
    add_over_y(r_ref, out_ref)
    out_ref[NX * BLOCK :, :] = later_ref[(j - 1) * NX * BLOCK : j * NX * BLOCK, :]


def far(x):
    return x // (NX // 2)


def place(r_ref, offset, vec_ref, crossed=False):
    side = far(lax.axis_index("x"))
    for x in range(NX):
        for k in range(NCORE):
            at = (x * NCORE + k) * BLOCK
            vec_ref[at : at + BLOCK, :] = r_ref[(side + far(x) + k) % NCORE if crossed else k, offset + x * BLOCK : offset + (x + 1) * BLOCK, :]
    return vec_ref[...]


def whole_index():
    return lax.broadcasted_iota(jnp.int32, (FULL, LANES), 0) * LANES + lax.broadcasted_iota(
        jnp.int32, (FULL, LANES), 1
    )


def householder(column, j):
    index = whole_index()
    below = index > j + 1
    squares = total(jnp.where(below, column * column, 0.0))
    pivot = column[0:1, j + 1 : j + 2]
    length = jnp.sqrt(pivot * pivot + squares)
    beta = jnp.where(pivot >= 0, -length, length)
    divisor = pivot - beta
    reflect = jnp.where(below, column / divisor, 0.0) + (index == j + 1).astype(f32)
    return reflect, (beta - pivot) / beta, divisor, jnp.where(below, column, 0.0)


def multiply(held, parts, sums):
    for block in range(BLOCK):
        rows = slice(block * LANES, (block + 1) * LANES)
        acc = held[rows, :LANES] * parts[0]
        for n in range(1, WIDE):
            acc = acc + held[rows, n * LANES : (n + 1) * LANES] * parts[n]
        sums[block : block + 1, :] = jnp.sum(acc.T, axis=0, keepdims=True)
    return sums[...]


def place_of_columns():
    return (lax.axis_index("z") * NY + lax.axis_index("y")) * WIDE


def first_step(r_ref, held, x_out, sums):
    index = (
        place_of_columns() + lax.broadcasted_iota(jnp.int32, (WIDE, LANES), 0)
    ) * LANES + lax.broadcasted_iota(jnp.int32, (WIDE, LANES), 1)
    below = jnp.where(index > 1, r_ref[:WIDE, :], 0.0)
    product = multiply(held, [below[n : n + 1, :] for n in range(WIDE)], sums)
    for d in range(NZ):
        x_out[d, :BLOCK, :] = product
        x_out[d, BLOCK : BLOCK + SLICE, :] = r_ref[WIDE : WIDE + SLICE, :]


def step(j, *refs):
    refs = list(refs)
    take = lambda count: [refs.pop(0) for _ in range(count)]
    r_ref, held = take(2)
    s_in, v_in, y_in = take(j > 1), take(j if j > 1 else 0), take(j - 1)
    v_out, s_out, x_out, y_out = take(4)
    v_first = take(j == 1)
    vec_ref, sums = take(2)

    line = lax.broadcasted_iota(jnp.int32, (8, LANES), 0)
    lane = lax.broadcasted_iota(jnp.int32, (8, LANES), 1)
    vs = [v[...] for v in v_in]
    ys = [y[...] for y in y_in]
    product = place(r_ref, 0, vec_ref, j > 1)
    column = place(r_ref, NX * BLOCK, vec_ref)
    if j == 1:
        reflect, tau, divisor, _ = householder(place(r_ref, 2 * NX * BLOCK, vec_ref), 0)
        state = jnp.where((line == 0) & (lane == 0), tau, 0.0)
        vs.append(reflect)
        v_first[0][...] = reflect
    else:
        state = s_in[0][...]
        divisor = state[7:8, j - 1 : j]
    product = product / divisor + column
    if j > 1:
        for i in range(j - 1):
            product = product - state[4 + i : 5 + i, j - 1 : j] * ys[i]
    ys.append(state[j - 1 : j, j - 1 : j] * product)
    y_out[...] = ys[j - 1]
    for i in range(j):
        column = column - vs[i][0:1, j : j + 1] * ys[i]
    dots = [total(v * column) for v in vs]
    for k in range(j):
        weight = state[0:1, k : k + 1] * dots[0]
        for i in range(1, k + 1):
            weight = weight + state[i : i + 1, k : k + 1] * dots[i]
        column = column - weight * vs[k]
    reflect, tau, divisor, undivided = householder(column, j)
    vec_ref[...] = reflect if j == K - 1 else undivided
    v_out[...] = reflect

    crosses = [total(v * reflect) for v in vs]
    old = state
    for i in range(j):
        entry = old[i : i + 1, i : i + 1] * crosses[i]
        for k in range(i + 1, j):
            entry = entry + old[i : i + 1, k : k + 1] * crosses[k]
        state = jnp.where((line == i) & (lane == j), -tau * entry, state)
        state = jnp.where((line == 4 + i) & (lane == j), crosses[i], state)
    state = jnp.where((line == 7) & (lane == j), divisor, state)
    s_out[...] = jnp.where((line == j) & (lane == j), tau, state)

    mine = place_of_columns()
    product = multiply(held, [vec_ref[pl.ds(mine + n, 1), :] for n in range(WIDE)], sums)
    for d in range(NZ * NY if j == K - 1 else NZ):
        x_out[d] = product


def finish(r_ref, s_in, *refs):
    v_in, y_in, (y_out, v_out, t_out) = refs[:K], refs[K : 2 * K - 1], refs[2 * K - 1 :]
    at = (lax.axis_index("x") * NCORE + lax.axis_index("core")) * BLOCK
    at = pl.multiple_of(at, 8)
    state = s_in[...]
    product = r_ref[0]
    for d in range(1, NZ * NY):
        product = product + r_ref[d]
    ys = [y[pl.ds(at, BLOCK), :] for y in y_in]
    for i in range(K - 1):
        product = product - state[4 + i : 5 + i, K - 1 : K] * ys[i]
    ys.append(state[K - 1 : K, K - 1 : K] * product)
    for i in range(K):
        v = v_in[i][pl.ds(at, BLOCK), :]
        for n in range(BLOCK):
            y_out[i : i + 1, n * LANES : (n + 1) * LANES] = ys[i][n : n + 1, :]
            v_out[i : i + 1, n * LANES : (n + 1) * LANES] = v[n : n + 1, :]
    t_out[...] = state[0:K, 0:K]


def swap(value, axes):
    return lax.all_to_all(value, axes, 0, 0, tiled=True)


def swap_across(value):
    place_of = lambda x, k, z, y: ((x * NCORE + k) * NZ + z) * NY + y
    groups = [
        [place_of(x, (k + far(x)) % NCORE, z, y) for x in range(NX) for y in range(NY)]
        for k in range(NCORE)
        for z in range(NZ)
    ]
    return lax.all_to_all(value, ("x", "core", "z", "y"), 0, 0, axis_index_groups=groups, tiled=True)


def call(kernel, ins, outs, scratch=(), mib=8, **more):
    return pl.pallas_call(
        kernel,
        in_specs=[VMEM] * len(ins),
        out_specs=[VMEM] * len(outs),
        out_shape=[vec(*shape) for shape in outs],
        scratch_shapes=[pltpu.VMEM(shape, f32) for shape in scratch],
        compiler_params=params(mib),
        **more,
    )(*ins)


def spread_panel(matrix):
    cols, sent = pl.pallas_call(
        take_panel,
        in_specs=[pl.BlockSpec(memory_space=pl.ANY)],
        out_specs=[VMEM] * 2,
        out_shape=[vec(K, BLOCK, LANES), vec(NX * NCORE, BLOCK, LANES)],
        scratch_shapes=[pltpu.VMEM((matrix.shape[0], LANES), f32), pltpu.SemaphoreType.DMA((CHUNKS,))],
        compiler_params=params(48),
    )(matrix)
    return call(
        pack_panel,
        [swap(sent, ("x", "core")), cols],
        [(NZ * NY, 1, (WIDE + SLICE) * LANES)],
    )[0]


def on_device(matrix):
    rows_dev, cols_dev = matrix.shape

    sent = lax.cond(
        (lax.axis_index("z") == 0) & (lax.axis_index("y") == 0),
        spread_panel,
        lambda _: jnp.zeros((NZ * NY, 1, (WIDE + SLICE) * LANES), f32),
        matrix,
    )
    (mine,) = call(
        pick_panel,
        [swap(sent, ("z", "y"))],
        [(16, LANES)],
        cost_estimate=pl.CostEstimate(flops=1 << 32, bytes_accessed=1 << 20, transcendentals=0),
    )
    (sent,) = call(first_step, [mine, matrix], [(NZ, 32, LANES)], [(BLOCK, LANES)])
    (sent,) = call(pass_first, [swap(sent, "z")], [(GROUP, 2 * BLOCK, LANES)], [(2 * BLOCK, LANES)])
    mine, later = call(
        pick_first, [swap(sent, ("x", "y"))], [(3 * NX * BLOCK, LANES), (2 * NX * BLOCK, LANES)]
    )
    state, vs, ys = [], [], []
    for j in range(1, K):
        got = lax.all_gather(mine, "core")
        send = (NZ * NY if j == K - 1 else NZ, BLOCK, LANES)
        whole = (FULL, LANES)
        v, s, sent, y, *first = call(
            functools.partial(step, j),
            [got, matrix, *state, *vs, *ys],
            [whole, (8, LANES), send, whole] + [whole] * (j == 1),
            [whole, (BLOCK, LANES)],
        )
        state, vs, ys = [s], [*first, *vs, v], [*ys, y]
        if j < K - 1:
            (sent,) = call(pass_product, [swap(sent, "z")], [(GROUP, BLOCK, LANES)], [(BLOCK, LANES)])
            (mine,) = call(
                functools.partial(pick_product, j),
                [swap_across(sent), later],
                [(2 * NX * BLOCK, LANES)],
            )
    got = swap(sent, ("z", "y"))
    return call(finish, [got, *state, *vs, *ys], [(K, rows_dev), (K, rows_dev), (K, K)])


def solution(mesh):
    grid = Mesh(mesh.devices.reshape(NX, NCORE, NZ, NY), ("x", "core", "z", "y"))
    return jax.shard_map(
        on_device,
        mesh=grid,
        in_specs=(P(("x", "core"), ("z", "y")),),
        out_specs=(P(None, ("x", "core")), P(None, ("x", "core")), P()),
        check_vma=False,
    )
```

```python
import functools

import jax
import jax.numpy as jnp
from jax import lax
from jax.experimental import pallas as pl
from jax.experimental.pallas import tpu as pltpu
from jax.sharding import Mesh, PartitionSpec as P

K = 4
LANES = 128
NX, NCORE, NZ, NY = 4, 2, 8, 4
GROUP = NX * NY
BLOCK = 24
FULL = NX * NCORE * BLOCK
SLICE = BLOCK // NZ
CHUNKS = 4
WIDE = 6

f32 = jnp.float32
VMEM = pl.BlockSpec(memory_space=pltpu.VMEM)


def params(mib):
    return pltpu.CompilerParams(vmem_limit_bytes=mib << 20)


def vec(*shape):
    return jax.ShapeDtypeStruct(shape, f32)


def total(value):
    return jnp.sum(jnp.sum(value, axis=0, keepdims=True), axis=1, keepdims=True)


def take_panel(a_ref, cols_ref, out_ref, slab, sems):
    rows = slab.shape[0] // CHUNKS
    copies = []
    for n in range(CHUNKS):
        part = pl.ds(n * rows, rows)
        copies.append(pltpu.make_async_copy(a_ref.at[part, pl.ds(0, LANES)], slab.at[part, :], sems.at[n]))
        copies[n].start()
    for block in range(BLOCK):
        if block % (BLOCK // CHUNKS) == 0:
            copies[block // (BLOCK // CHUNKS)].wait()
        turned = slab[block * LANES : (block + 1) * LANES, :].T
        for i in range(K):
            cols_ref[i, block : block + 1, :] = turned[i : i + 1, :]
    for d in range(NX * NCORE):
        out_ref[d] = cols_ref[0]


def pack_panel(r_ref, cols_ref, out_ref):
    for z in range(NZ):
        for y in range(NY):
            d = z * NY + y
            for n in range(WIDE):
                out_ref[d, :, n * LANES : (n + 1) * LANES] = r_ref[z, WIDE * y + n : WIDE * y + n + 1, :]
            for n in range(SLICE):
                at = (WIDE + n) * LANES
                out_ref[d, :, at : at + LANES] = cols_ref[y, SLICE * z + n : SLICE * z + n + 1, :]


def pick_panel(r_ref, out_ref):
    for n in range(WIDE + SLICE):
        out_ref[n : n + 1, :] = r_ref[0, :, n * LANES : (n + 1) * LANES]


def add_over_z(r_ref, stage):
    sums = r_ref[0, :BLOCK, :]
    for z in range(1, NZ):
        sums = sums + r_ref[z, :BLOCK, :]
    stage[:BLOCK, :] = sums


def pass_first(r_ref, out_ref, stage):
    add_over_z(r_ref, stage)
    for z in range(NZ):
        stage[BLOCK + SLICE * z : BLOCK + SLICE * (z + 1), :] = r_ref[z, BLOCK : BLOCK + SLICE, :]
    for d in range(GROUP):
        out_ref[d] = stage[...]


def pass_product(r_ref, out_ref, stage):
    add_over_z(r_ref, stage)
    for d in range(GROUP):
        out_ref[d] = stage[...]


def add_over_y(r_ref, out_ref):
    for x in range(NX):
        sums = r_ref[x * NY, :BLOCK, :]
        for y in range(1, NY):
            sums = sums + r_ref[x * NY + y, :BLOCK, :]
        out_ref[x * BLOCK : (x + 1) * BLOCK, :] = sums


def pick_first(r_ref, out_ref, later_ref):
    add_over_y(r_ref, out_ref)
    for x in range(NX):
        for y in range(NY):
            block = r_ref[x * NY + y, BLOCK:, :]
            if y < 2:
                at = (2 - y) * NX * BLOCK + x * BLOCK
                out_ref[at : at + BLOCK, :] = block
            else:
                at = (y - 2) * NX * BLOCK + x * BLOCK
                later_ref[at : at + BLOCK, :] = block


def pick_product(j, r_ref, later_ref, out_ref):
    add_over_y(r_ref, out_ref)
    out_ref[NX * BLOCK :, :] = later_ref[(j - 1) * NX * BLOCK : j * NX * BLOCK, :]


def far(x):
    return x // (NX // 2)


def place(r_ref, offset, vec_ref, crossed=False):
    side = far(lax.axis_index("x"))
    for x in range(NX):
        for k in range(NCORE):
            at = (x * NCORE + k) * BLOCK
            vec_ref[at : at + BLOCK, :] = r_ref[(side + far(x) + k) % NCORE if crossed else k, offset + x * BLOCK : offset + (x + 1) * BLOCK, :]
    return vec_ref[...]


def whole_index():
    return lax.broadcasted_iota(jnp.int32, (FULL, LANES), 0) * LANES + lax.broadcasted_iota(
        jnp.int32, (FULL, LANES), 1
    )


def householder(column, j):
    index = whole_index()
    below = index > j + 1
    squares = total(jnp.where(below, column * column, 0.0))
    pivot = column[0:1, j + 1 : j + 2]
    length = jnp.sqrt(pivot * pivot + squares)
    beta = jnp.where(pivot >= 0, -length, length)
    divisor = pivot - beta
    reflect = jnp.where(below, column / divisor, 0.0) + (index == j + 1).astype(f32)
    return reflect, (beta - pivot) / beta, divisor, jnp.where(below, column, 0.0)


def multiply(held, parts, sums):
    for block in range(BLOCK):
        rows = slice(block * LANES, (block + 1) * LANES)
        acc = held[rows, :LANES] * parts[0]
        for n in range(1, WIDE):
            acc = acc + held[rows, n * LANES : (n + 1) * LANES] * parts[n]
        sums[block : block + 1, :] = jnp.sum(acc.T, axis=0, keepdims=True)
    return sums[...]


def place_of_columns():
    return (lax.axis_index("z") * NY + lax.axis_index("y")) * WIDE


def first_step(r_ref, held, x_out, sums):
    index = (
        place_of_columns() + lax.broadcasted_iota(jnp.int32, (WIDE, LANES), 0)
    ) * LANES + lax.broadcasted_iota(jnp.int32, (WIDE, LANES), 1)
    below = jnp.where(index > 1, r_ref[:WIDE, :], 0.0)
    product = multiply(held, [below[n : n + 1, :] for n in range(WIDE)], sums)
    for d in range(NZ):
        x_out[d, :BLOCK, :] = product
        x_out[d, BLOCK : BLOCK + SLICE, :] = r_ref[WIDE : WIDE + SLICE, :]


def step(j, *refs):
    refs = list(refs)
    take = lambda count: [refs.pop(0) for _ in range(count)]
    r_ref, held = take(2)
    s_in, v_in, y_in = take(j > 1), take(j if j > 1 else 0), take(j - 1)
    v_out, s_out, x_out, y_out = take(4)
    v_first = take(j == 1)
    vec_ref, sums = take(2)

    line = lax.broadcasted_iota(jnp.int32, (8, LANES), 0)
    lane = lax.broadcasted_iota(jnp.int32, (8, LANES), 1)
    vs = [v[...] for v in v_in]
    ys = [y[...] for y in y_in]
    product = place(r_ref, 0, vec_ref, j > 1)
    column = place(r_ref, NX * BLOCK, vec_ref)
    if j == 1:
        reflect, tau, divisor, _ = householder(place(r_ref, 2 * NX * BLOCK, vec_ref), 0)
        state = jnp.where((line == 0) & (lane == 0), tau, 0.0)
        vs.append(reflect)
        v_first[0][...] = reflect
    else:
        state = s_in[0][...]
        divisor = state[7:8, j - 1 : j]
    product = product / divisor + column
    if j > 1:
        for i in range(j - 1):
            product = product - state[4 + i : 5 + i, j - 1 : j] * ys[i]
    ys.append(state[j - 1 : j, j - 1 : j] * product)
    y_out[...] = ys[j - 1]
    for i in range(j):
        column = column - vs[i][0:1, j : j + 1] * ys[i]
    dots = [total(v * column) for v in vs]
    for k in range(j):
        weight = state[0:1, k : k + 1] * dots[0]
        for i in range(1, k + 1):
            weight = weight + state[i : i + 1, k : k + 1] * dots[i]
        column = column - weight * vs[k]
    reflect, tau, divisor, undivided = householder(column, j)
    vec_ref[...] = reflect if j == K - 1 else undivided
    v_out[...] = reflect

    crosses = [total(v * reflect) for v in vs]
    old = state
    for i in range(j):
        entry = old[i : i + 1, i : i + 1] * crosses[i]
        for k in range(i + 1, j):
            entry = entry + old[i : i + 1, k : k + 1] * crosses[k]
        state = jnp.where((line == i) & (lane == j), -tau * entry, state)
        state = jnp.where((line == 4 + i) & (lane == j), crosses[i], state)
    state = jnp.where((line == 7) & (lane == j), divisor, state)
    s_out[...] = jnp.where((line == j) & (lane == j), tau, state)

    mine = place_of_columns()
    product = multiply(held, [vec_ref[pl.ds(mine + n, 1), :] for n in range(WIDE)], sums)
    for d in range(NZ * NY if j == K - 1 else NZ):
        x_out[d] = product


def finish(r_ref, s_in, *refs):
    v_in, y_in, (y_out, v_out, t_out) = refs[:K], refs[K : 2 * K - 1], refs[2 * K - 1 :]
    at = (lax.axis_index("x") * NCORE + lax.axis_index("core")) * BLOCK
    at = pl.multiple_of(at, 8)
    state = s_in[...]
    product = r_ref[0]
    for d in range(1, NZ * NY):
        product = product + r_ref[d]
    ys = [y[pl.ds(at, BLOCK), :] for y in y_in]
    for i in range(K - 1):
        product = product - state[4 + i : 5 + i, K - 1 : K] * ys[i]
    ys.append(state[K - 1 : K, K - 1 : K] * product)
    for i in range(K):
        v = v_in[i][pl.ds(at, BLOCK), :]
        for n in range(BLOCK):
            y_out[i : i + 1, n * LANES : (n + 1) * LANES] = ys[i][n : n + 1, :]
            v_out[i : i + 1, n * LANES : (n + 1) * LANES] = v[n : n + 1, :]
    t_out[...] = state[0:K, 0:K]


def swap(value, axes):
    return lax.all_to_all(value, axes, 0, 0, tiled=True)


def swap_across(value):
    place_of = lambda x, k, z, y: ((x * NCORE + k) * NZ + z) * NY + y
    groups = [
        [place_of(x, (k + far(x)) % NCORE, z, y) for x in range(NX) for y in range(NY)]
        for k in range(NCORE)
        for z in range(NZ)
    ]
    return lax.all_to_all(value, ("x", "core", "z", "y"), 0, 0, axis_index_groups=groups, tiled=True)


def call(kernel, ins, outs, scratch=(), mib=8, **more):
    return pl.pallas_call(
        kernel,
        in_specs=[VMEM] * len(ins),
        out_specs=[VMEM] * len(outs),
        out_shape=[vec(*shape) for shape in outs],
        scratch_shapes=[pltpu.VMEM(shape, f32) for shape in scratch],
        compiler_params=params(mib),
        **more,
    )(*ins)


def spread_panel(matrix):
    cols, sent = pl.pallas_call(
        take_panel,
        in_specs=[pl.BlockSpec(memory_space=pl.ANY)],
        out_specs=[VMEM] * 2,
        out_shape=[vec(K, BLOCK, LANES), vec(NX * NCORE, BLOCK, LANES)],
        scratch_shapes=[pltpu.VMEM((matrix.shape[0], LANES), f32), pltpu.SemaphoreType.DMA((CHUNKS,))],
        compiler_params=params(48),
    )(matrix)
    return call(
        pack_panel,
        [swap(sent, ("x", "core")), cols],
        [(NZ * NY, 1, (WIDE + SLICE) * LANES)],
    )[0]


def on_device(matrix):
    rows_dev, cols_dev = matrix.shape

    sent = lax.cond(
        (lax.axis_index("z") == 0) & (lax.axis_index("y") == 0),
        spread_panel,
        lambda _: jnp.zeros((NZ * NY, 1, (WIDE + SLICE) * LANES), f32),
        matrix,
    )
    (mine,) = call(
        pick_panel,
        [swap(sent, ("z", "y"))],
        [(16, LANES)],
        cost_estimate=pl.CostEstimate(flops=1 << 32, bytes_accessed=1 << 20, transcendentals=0),
    )
    (sent,) = call(first_step, [mine, matrix], [(NZ, 32, LANES)], [(BLOCK, LANES)])
    (sent,) = call(pass_first, [swap(sent, "z")], [(GROUP, 2 * BLOCK, LANES)], [(2 * BLOCK, LANES)])
    mine, later = call(
        pick_first, [swap(sent, ("x", "y"))], [(3 * NX * BLOCK, LANES), (2 * NX * BLOCK, LANES)]
    )
    state, vs, ys = [], [], []
    for j in range(1, K):
        got = lax.all_gather(mine, "core")
        send = (NZ * NY if j == K - 1 else NZ, BLOCK, LANES)
        whole = (FULL, LANES)
        v, s, sent, y, *first = call(
            functools.partial(step, j),
            [got, matrix, *state, *vs, *ys],
            [whole, (8, LANES), send, whole] + [whole] * (j == 1),
            [whole, (BLOCK, LANES)],
        )
        state, vs, ys = [s], [*first, *vs, v], [*ys, y]
        if j < K - 1:
            (sent,) = call(pass_product, [swap(sent, "z")], [(GROUP, BLOCK, LANES)], [(BLOCK, LANES)])
            (mine,) = call(
                functools.partial(pick_product, j),
                [swap_across(sent), later],
                [(2 * NX * BLOCK, LANES)],
            )
    got = swap(sent, ("z", "y"))
    return call(finish, [got, *state, *vs, *ys], [(K, rows_dev), (K, rows_dev), (K, K)])


def solution(mesh):
    grid = Mesh(mesh.devices.reshape(NX, NCORE, NZ, NY), ("x", "core", "z", "y"))
    return jax.shard_map(
        on_device,
        mesh=grid,
        in_specs=(P(("x", "core"), ("z", "y")),),
        out_specs=(P(None, ("x", "core")), P(None, ("x", "core")), P()),
        check_vma=False,
    )
```

```python
import functools

import jax
import jax.numpy as jnp
from jax import lax
from jax.experimental import pallas as pl
from jax.experimental.pallas import tpu as pltpu
from jax.sharding import Mesh, PartitionSpec as P

K = 4
LANES = 128
NX, NCORE, NZ, NY = 4, 2, 8, 4
GROUP = NX * NY
BLOCK = 24
FULL = NX * NCORE * BLOCK
SLICE = BLOCK // NZ
CHUNKS = 4
WIDE = 6

f32 = jnp.float32
VMEM = pl.BlockSpec(memory_space=pltpu.VMEM)


def params(mib):
    return pltpu.CompilerParams(vmem_limit_bytes=mib << 20)


def vec(*shape):
    return jax.ShapeDtypeStruct(shape, f32)


def total(value):
    return jnp.sum(jnp.sum(value, axis=0, keepdims=True), axis=1, keepdims=True)


def take_panel(a_ref, cols_ref, out_ref, slab, sems):
    rows = slab.shape[0] // CHUNKS
    copies = []
    for n in range(CHUNKS):
        part = pl.ds(n * rows, rows)
        copies.append(pltpu.make_async_copy(a_ref.at[part, pl.ds(0, LANES)], slab.at[part, :], sems.at[n]))
        copies[n].start()
    for block in range(BLOCK):
        if block % (BLOCK // CHUNKS) == 0:
            copies[block // (BLOCK // CHUNKS)].wait()
        turned = slab[block * LANES : (block + 1) * LANES, :].T
        for i in range(K):
            cols_ref[i, block : block + 1, :] = turned[i : i + 1, :]
    for d in range(NX * NCORE):
        out_ref[d] = cols_ref[0]


def pack_panel(r_ref, cols_ref, out_ref):
    for z in range(NZ):
        for y in range(NY):
            d = z * NY + y
            for n in range(WIDE):
                out_ref[d, :, n * LANES : (n + 1) * LANES] = r_ref[z, WIDE * y + n : WIDE * y + n + 1, :]
            for n in range(SLICE):
                at = (WIDE + n) * LANES
                out_ref[d, :, at : at + LANES] = cols_ref[y, SLICE * z + n : SLICE * z + n + 1, :]


def pick_panel(r_ref, out_ref):
    for n in range(WIDE + SLICE):
        out_ref[n : n + 1, :] = r_ref[0, :, n * LANES : (n + 1) * LANES]


def add_over_z(r_ref, stage):
    sums = r_ref[0, :BLOCK, :]
    for z in range(1, NZ):
        sums = sums + r_ref[z, :BLOCK, :]
    stage[:BLOCK, :] = sums


def pass_first(r_ref, out_ref, stage):
    add_over_z(r_ref, stage)
    for z in range(NZ):
        stage[BLOCK + SLICE * z : BLOCK + SLICE * (z + 1), :] = r_ref[z, BLOCK : BLOCK + SLICE, :]
    for d in range(GROUP):
        out_ref[d] = stage[...]


def pass_product(r_ref, out_ref, stage):
    add_over_z(r_ref, stage)
    for d in range(out_ref.shape[0]):
        out_ref[d] = stage[...]


def add_over_y(r_ref, out_ref):
    for x in range(NX):
        sums = r_ref[x * NY, :BLOCK, :]
        for y in range(1, NY):
            sums = sums + r_ref[x * NY + y, :BLOCK, :]
        out_ref[x * BLOCK : (x + 1) * BLOCK, :] = sums


def pick_first(r_ref, out_ref, later_ref):
    add_over_y(r_ref, out_ref)
    for x in range(NX):
        for y in range(NY):
            block = r_ref[x * NY + y, BLOCK:, :]
            if y < 2:
                at = (2 - y) * NX * BLOCK + x * BLOCK
                out_ref[at : at + BLOCK, :] = block
            else:
                at = (y - 2) * NX * BLOCK + x * BLOCK
                later_ref[at : at + BLOCK, :] = block


def pick_product(j, r_ref, later_ref, out_ref):
    add_over_y(r_ref, out_ref)
    out_ref[NX * BLOCK :, :] = later_ref[(j - 1) * NX * BLOCK : j * NX * BLOCK, :]


def far(x):
    return x // (NX // 2)


def place(r_ref, offset, vec_ref, crossed=False):
    side = far(lax.axis_index("x"))
    for x in range(NX):
        for k in range(NCORE):
            at = (x * NCORE + k) * BLOCK
            vec_ref[at : at + BLOCK, :] = r_ref[(side + far(x) + k) % NCORE if crossed else k, offset + x * BLOCK : offset + (x + 1) * BLOCK, :]
    return vec_ref[...]


def whole_index():
    return lax.broadcasted_iota(jnp.int32, (FULL, LANES), 0) * LANES + lax.broadcasted_iota(
        jnp.int32, (FULL, LANES), 1
    )


def householder(column, j):
    index = whole_index()
    below = index > j + 1
    squares = total(jnp.where(below, column * column, 0.0))
    pivot = column[0:1, j + 1 : j + 2]
    length = jnp.sqrt(pivot * pivot + squares)
    beta = jnp.where(pivot >= 0, -length, length)
    divisor = pivot - beta
    reflect = jnp.where(below, column / divisor, 0.0) + (index == j + 1).astype(f32)
    return reflect, (beta - pivot) / beta, divisor, jnp.where(below, column, 0.0)


def multiply(held, parts, sums):
    for block in range(BLOCK):
        rows = slice(block * LANES, (block + 1) * LANES)
        acc = held[rows, :LANES] * parts[0]
        for n in range(1, WIDE):
            acc = acc + held[rows, n * LANES : (n + 1) * LANES] * parts[n]
        sums[block : block + 1, :] = jnp.sum(acc.T, axis=0, keepdims=True)
    return sums[...]


def place_of_columns():
    return (lax.axis_index("z") * NY + lax.axis_index("y")) * WIDE


def first_step(r_ref, held, x_out, sums):
    index = (
        place_of_columns() + lax.broadcasted_iota(jnp.int32, (WIDE, LANES), 0)
    ) * LANES + lax.broadcasted_iota(jnp.int32, (WIDE, LANES), 1)
    below = jnp.where(index > 1, r_ref[:WIDE, :], 0.0)
    product = multiply(held, [below[n : n + 1, :] for n in range(WIDE)], sums)
    for d in range(NZ):
        x_out[d, :BLOCK, :] = product
        x_out[d, BLOCK : BLOCK + SLICE, :] = r_ref[WIDE : WIDE + SLICE, :]


def step(j, *refs):
    refs = list(refs)
    take = lambda count: [refs.pop(0) for _ in range(count)]
    r_ref, held = take(2)
    s_in, v_in, y_in = take(j > 1), take(j if j > 1 else 0), take(j - 1)
    v_out, s_out, x_out, y_out = take(4)
    v_first = take(j == 1)
    vec_ref, sums = take(2)

    line = lax.broadcasted_iota(jnp.int32, (8, LANES), 0)
    lane = lax.broadcasted_iota(jnp.int32, (8, LANES), 1)
    vs = [v[...] for v in v_in]
    ys = [y[...] for y in y_in]
    product = place(r_ref, 0, vec_ref, j > 1)
    column = place(r_ref, NX * BLOCK, vec_ref)
    if j == 1:
        reflect, tau, divisor, _ = householder(place(r_ref, 2 * NX * BLOCK, vec_ref), 0)
        state = jnp.where((line == 0) & (lane == 0), tau, 0.0)
        vs.append(reflect)
        v_first[0][...] = reflect
    else:
        state = s_in[0][...]
        divisor = state[7:8, j - 1 : j]
    product = product / divisor + column
    if j > 1:
        for i in range(j - 1):
            product = product - state[4 + i : 5 + i, j - 1 : j] * ys[i]
    ys.append(state[j - 1 : j, j - 1 : j] * product)
    y_out[...] = ys[j - 1]
    for i in range(j):
        column = column - vs[i][0:1, j : j + 1] * ys[i]
    dots = [total(v * column) for v in vs]
    for k in range(j):
        weight = state[0:1, k : k + 1] * dots[0]
        for i in range(1, k + 1):
            weight = weight + state[i : i + 1, k : k + 1] * dots[i]
        column = column - weight * vs[k]
    reflect, tau, divisor, undivided = householder(column, j)
    vec_ref[...] = reflect if j == K - 1 else undivided
    v_out[...] = reflect

    crosses = [total(v * reflect) for v in vs]
    old = state
    for i in range(j):
        entry = old[i : i + 1, i : i + 1] * crosses[i]
        for k in range(i + 1, j):
            entry = entry + old[i : i + 1, k : k + 1] * crosses[k]
        state = jnp.where((line == i) & (lane == j), -tau * entry, state)
        state = jnp.where((line == 4 + i) & (lane == j), crosses[i], state)
    state = jnp.where((line == 7) & (lane == j), divisor, state)
    s_out[...] = jnp.where((line == j) & (lane == j), tau, state)

    mine = place_of_columns()
    product = multiply(held, [vec_ref[pl.ds(mine + n, 1), :] for n in range(WIDE)], sums)
    for d in range(NZ):
        x_out[d] = product


def finish(r_ref, s_in, *refs):
    v_in, y_in, (y_out, v_out, t_out) = refs[:K], refs[K : 2 * K - 1], refs[2 * K - 1 :]
    at = (lax.axis_index("x") * NCORE + lax.axis_index("core")) * BLOCK
    at = pl.multiple_of(at, 8)
    state = s_in[...]
    product = r_ref[0]
    for d in range(1, NY):
        product = product + r_ref[d]
    ys = [y[pl.ds(at, BLOCK), :] for y in y_in]
    for i in range(K - 1):
        product = product - state[4 + i : 5 + i, K - 1 : K] * ys[i]
    ys.append(state[K - 1 : K, K - 1 : K] * product)
    for i in range(K):
        v = v_in[i][pl.ds(at, BLOCK), :]
        for n in range(BLOCK):
            y_out[i : i + 1, n * LANES : (n + 1) * LANES] = ys[i][n : n + 1, :]
            v_out[i : i + 1, n * LANES : (n + 1) * LANES] = v[n : n + 1, :]
    t_out[...] = state[0:K, 0:K]


def swap(value, axes):
    return lax.all_to_all(value, axes, 0, 0, tiled=True)


def swap_across(value):
    place_of = lambda x, k, z, y: ((x * NCORE + k) * NZ + z) * NY + y
    groups = [
        [place_of(x, (k + far(x)) % NCORE, z, y) for x in range(NX) for y in range(NY)]
        for k in range(NCORE)
        for z in range(NZ)
    ]
    return lax.all_to_all(value, ("x", "core", "z", "y"), 0, 0, axis_index_groups=groups, tiled=True)


def call(kernel, ins, outs, scratch=(), mib=8, **more):
    return pl.pallas_call(
        kernel,
        in_specs=[VMEM] * len(ins),
        out_specs=[VMEM] * len(outs),
        out_shape=[vec(*shape) for shape in outs],
        scratch_shapes=[pltpu.VMEM(shape, f32) for shape in scratch],
        compiler_params=params(mib),
        **more,
    )(*ins)


def spread_panel(matrix):
    cols, sent = pl.pallas_call(
        take_panel,
        in_specs=[pl.BlockSpec(memory_space=pl.ANY)],
        out_specs=[VMEM] * 2,
        out_shape=[vec(K, BLOCK, LANES), vec(NX * NCORE, BLOCK, LANES)],
        scratch_shapes=[pltpu.VMEM((matrix.shape[0], LANES), f32), pltpu.SemaphoreType.DMA((CHUNKS,))],
        compiler_params=params(48),
    )(matrix)
    return call(
        pack_panel,
        [swap(sent, ("x", "core")), cols],
        [(NZ * NY, 1, (WIDE + SLICE) * LANES)],
    )[0]


def on_device(matrix):
    rows_dev, cols_dev = matrix.shape

    sent = lax.cond(
        (lax.axis_index("z") == 0) & (lax.axis_index("y") == 0),
        spread_panel,
        lambda _: jnp.zeros((NZ * NY, 1, (WIDE + SLICE) * LANES), f32),
        matrix,
    )
    (mine,) = call(
        pick_panel,
        [swap(sent, ("z", "y"))],
        [(16, LANES)],
        cost_estimate=pl.CostEstimate(flops=1 << 32, bytes_accessed=1 << 20, transcendentals=0),
    )
    (sent,) = call(first_step, [mine, matrix], [(NZ, 32, LANES)], [(BLOCK, LANES)])
    (sent,) = call(pass_first, [swap(sent, "z")], [(GROUP, 2 * BLOCK, LANES)], [(2 * BLOCK, LANES)])
    mine, later = call(
        pick_first, [swap(sent, ("x", "y"))], [(3 * NX * BLOCK, LANES), (2 * NX * BLOCK, LANES)]
    )
    state, vs, ys = [], [], []
    for j in range(1, K):
        got = lax.all_gather(mine, "core")
        send = (NZ, BLOCK, LANES)
        whole = (FULL, LANES)
        v, s, sent, y, *first = call(
            functools.partial(step, j),
            [got, matrix, *state, *vs, *ys],
            [whole, (8, LANES), send, whole] + [whole] * (j == 1),
            [whole, (BLOCK, LANES)],
        )
        state, vs, ys = [s], [*first, *vs, v], [*ys, y]
        if j < K - 1:
            (sent,) = call(pass_product, [swap(sent, "z")], [(GROUP, BLOCK, LANES)], [(BLOCK, LANES)])
            (mine,) = call(
                functools.partial(pick_product, j),
                [swap_across(sent), later],
                [(2 * NX * BLOCK, LANES)],
            )
    (sent,) = call(pass_product, [swap(sent, "z")], [(NY, BLOCK, LANES)], [(BLOCK, LANES)])
    got = swap(sent, "y")
    return call(finish, [got, *state, *vs, *ys], [(K, rows_dev), (K, rows_dev), (K, K)])


def solution(mesh):
    grid = Mesh(mesh.devices.reshape(NX, NCORE, NZ, NY), ("x", "core", "z", "y"))
    return jax.shard_map(
        on_device,
        mesh=grid,
        in_specs=(P(("x", "core"), ("z", "y")),),
        out_specs=(P(None, ("x", "core")), P(None, ("x", "core")), P()),
        check_vma=False,
    )
```

```python
import functools

import jax
import jax.numpy as jnp
from jax import lax
from jax.experimental import pallas as pl
from jax.experimental.pallas import tpu as pltpu
from jax.sharding import Mesh, PartitionSpec as P

K = 4
LANES = 128
NX, NCORE, NZ, NY = 4, 2, 8, 4
GROUP = NX * NY
BLOCK = 24
FULL = NX * NCORE * BLOCK
SLICE = BLOCK // NZ
CHUNKS = 4
WIDE = 6

f32 = jnp.float32
VMEM = pl.BlockSpec(memory_space=pltpu.VMEM)


def params(mib):
    return pltpu.CompilerParams(vmem_limit_bytes=mib << 20)


def vec(*shape):
    return jax.ShapeDtypeStruct(shape, f32)


def total(value):
    return jnp.sum(jnp.sum(value, axis=0, keepdims=True), axis=1, keepdims=True)


def take_panel(a_ref, cols_ref, out_ref, slab, sems):
    rows = slab.shape[0] // CHUNKS
    copies = []
    for n in range(CHUNKS):
        part = pl.ds(n * rows, rows)
        copies.append(pltpu.make_async_copy(a_ref.at[part, pl.ds(0, LANES)], slab.at[part, :], sems.at[n]))
        copies[n].start()
    for block in range(BLOCK):
        if block % (BLOCK // CHUNKS) == 0:
            copies[block // (BLOCK // CHUNKS)].wait()
        turned = slab[block * LANES : (block + 1) * LANES, :].T
        for i in range(K):
            cols_ref[i, block : block + 1, :] = turned[i : i + 1, :]
    for d in range(NX * NCORE):
        out_ref[d] = cols_ref[0]


def pack_panel(r_ref, cols_ref, out_ref):
    for z in range(NZ):
        for y in range(NY):
            d = z * NY + y
            for n in range(WIDE):
                out_ref[d, :, n * LANES : (n + 1) * LANES] = r_ref[z, WIDE * y + n : WIDE * y + n + 1, :]
            for n in range(SLICE):
                at = (WIDE + n) * LANES
                out_ref[d, :, at : at + LANES] = cols_ref[y, SLICE * z + n : SLICE * z + n + 1, :]


def pick_panel(r_ref, out_ref):
    for n in range(WIDE + SLICE):
        out_ref[n : n + 1, :] = r_ref[0, :, n * LANES : (n + 1) * LANES]


def add_over_z(r_ref, stage):
    sums = r_ref[0, :BLOCK, :]
    for z in range(1, r_ref.shape[0]):
        sums = sums + r_ref[z, :BLOCK, :]
    stage[:BLOCK, :] = sums


def pass_first(r_ref, out_ref, stage):
    add_over_z(r_ref, stage)
    for z in range(NZ):
        stage[BLOCK + SLICE * z : BLOCK + SLICE * (z + 1), :] = r_ref[z, BLOCK : BLOCK + SLICE, :]
    for d in range(GROUP):
        out_ref[d] = stage[...]


def pass_product(r_ref, out_ref, stage):
    add_over_z(r_ref, stage)
    for d in range(out_ref.shape[0]):
        out_ref[d] = stage[...]


def add_over_y(r_ref, out_ref):
    for x in range(NX):
        sums = r_ref[x * NY, :BLOCK, :]
        for y in range(1, NY):
            sums = sums + r_ref[x * NY + y, :BLOCK, :]
        out_ref[x * BLOCK : (x + 1) * BLOCK, :] = sums


def pick_first(r_ref, out_ref, later_ref):
    add_over_y(r_ref, out_ref)
    for x in range(NX):
        for y in range(NY):
            block = r_ref[x * NY + y, BLOCK:, :]
            if y < 2:
                at = (2 - y) * NX * BLOCK + x * BLOCK
                out_ref[at : at + BLOCK, :] = block
            else:
                at = (y - 2) * NX * BLOCK + x * BLOCK
                later_ref[at : at + BLOCK, :] = block


def pick_product(j, r_ref, later_ref, out_ref):
    add_over_y(r_ref, out_ref)
    out_ref[NX * BLOCK :, :] = later_ref[(j - 1) * NX * BLOCK : j * NX * BLOCK, :]


def far(x):
    return x // (NX // 2)


def place(r_ref, offset, vec_ref, crossed=False):
    side = far(lax.axis_index("x"))
    for x in range(NX):
        for k in range(NCORE):
            at = (x * NCORE + k) * BLOCK
            vec_ref[at : at + BLOCK, :] = r_ref[(side + far(x) + k) % NCORE if crossed else k, offset + x * BLOCK : offset + (x + 1) * BLOCK, :]
    return vec_ref[...]


def whole_index():
    return lax.broadcasted_iota(jnp.int32, (FULL, LANES), 0) * LANES + lax.broadcasted_iota(
        jnp.int32, (FULL, LANES), 1
    )


def householder(column, j):
    index = whole_index()
    below = index > j + 1
    squares = total(jnp.where(below, column * column, 0.0))
    pivot = column[0:1, j + 1 : j + 2]
    length = jnp.sqrt(pivot * pivot + squares)
    beta = jnp.where(pivot >= 0, -length, length)
    divisor = pivot - beta
    reflect = jnp.where(below, column / divisor, 0.0) + (index == j + 1).astype(f32)
    return reflect, (beta - pivot) / beta, divisor, jnp.where(below, column, 0.0)


def multiply(held, parts, sums):
    for block in range(BLOCK):
        rows = slice(block * LANES, (block + 1) * LANES)
        acc = held[rows, :LANES] * parts[0]
        for n in range(1, WIDE):
            acc = acc + held[rows, n * LANES : (n + 1) * LANES] * parts[n]
        sums[block : block + 1, :] = jnp.sum(acc.T, axis=0, keepdims=True)
    return sums[...]


def place_of_columns():
    return (lax.axis_index("z") * NY + lax.axis_index("y")) * WIDE


def first_step(r_ref, held, x_out, sums):
    index = (
        place_of_columns() + lax.broadcasted_iota(jnp.int32, (WIDE, LANES), 0)
    ) * LANES + lax.broadcasted_iota(jnp.int32, (WIDE, LANES), 1)
    below = jnp.where(index > 1, r_ref[:WIDE, :], 0.0)
    product = multiply(held, [below[n : n + 1, :] for n in range(WIDE)], sums)
    for d in range(NZ):
        x_out[d, :BLOCK, :] = product
        x_out[d, BLOCK : BLOCK + SLICE, :] = r_ref[WIDE : WIDE + SLICE, :]


def step(j, *refs):
    refs = list(refs)
    take = lambda count: [refs.pop(0) for _ in range(count)]
    r_ref, held = take(2)
    s_in, v_in, y_in = take(j > 1), take(j if j > 1 else 0), take(j - 1)
    v_out, s_out, x_out, y_out = take(4)
    v_first = take(j == 1)
    vec_ref, sums = take(2)

    line = lax.broadcasted_iota(jnp.int32, (8, LANES), 0)
    lane = lax.broadcasted_iota(jnp.int32, (8, LANES), 1)
    vs = [v[...] for v in v_in]
    ys = [y[...] for y in y_in]
    product = place(r_ref, 0, vec_ref, j > 1)
    column = place(r_ref, NX * BLOCK, vec_ref)
    if j == 1:
        reflect, tau, divisor, _ = householder(place(r_ref, 2 * NX * BLOCK, vec_ref), 0)
        state = jnp.where((line == 0) & (lane == 0), tau, 0.0)
        vs.append(reflect)
        v_first[0][...] = reflect
    else:
        state = s_in[0][...]
        divisor = state[7:8, j - 1 : j]
    product = product / divisor + column
    if j > 1:
        for i in range(j - 1):
            product = product - state[4 + i : 5 + i, j - 1 : j] * ys[i]
    ys.append(state[j - 1 : j, j - 1 : j] * product)
    y_out[...] = ys[j - 1]
    for i in range(j):
        column = column - vs[i][0:1, j : j + 1] * ys[i]
    dots = [total(v * column) for v in vs]
    for k in range(j):
        weight = state[0:1, k : k + 1] * dots[0]
        for i in range(1, k + 1):
            weight = weight + state[i : i + 1, k : k + 1] * dots[i]
        column = column - weight * vs[k]
    reflect, tau, divisor, undivided = householder(column, j)
    vec_ref[...] = reflect if j == K - 1 else undivided
    v_out[...] = reflect

    crosses = [total(v * reflect) for v in vs]
    old = state
    for i in range(j):
        entry = old[i : i + 1, i : i + 1] * crosses[i]
        for k in range(i + 1, j):
            entry = entry + old[i : i + 1, k : k + 1] * crosses[k]
        state = jnp.where((line == i) & (lane == j), -tau * entry, state)
        state = jnp.where((line == 4 + i) & (lane == j), crosses[i], state)
    state = jnp.where((line == 7) & (lane == j), divisor, state)
    s_out[...] = jnp.where((line == j) & (lane == j), tau, state)

    mine = place_of_columns()
    product = multiply(held, [vec_ref[pl.ds(mine + n, 1), :] for n in range(WIDE)], sums)
    for d in range(NY if j == K - 1 else NZ):
        x_out[d] = product


def finish(r_ref, s_in, *refs):
    v_in, y_in, (y_out, v_out, t_out) = refs[:K], refs[K : 2 * K - 1], refs[2 * K - 1 :]
    at = (lax.axis_index("x") * NCORE + lax.axis_index("core")) * BLOCK
    at = pl.multiple_of(at, 8)
    state = s_in[...]
    product = r_ref[0]
    for d in range(1, NZ):
        product = product + r_ref[d]
    ys = [y[pl.ds(at, BLOCK), :] for y in y_in]
    for i in range(K - 1):
        product = product - state[4 + i : 5 + i, K - 1 : K] * ys[i]
    ys.append(state[K - 1 : K, K - 1 : K] * product)
    for i in range(K):
        v = v_in[i][pl.ds(at, BLOCK), :]
        for n in range(BLOCK):
            y_out[i : i + 1, n * LANES : (n + 1) * LANES] = ys[i][n : n + 1, :]
            v_out[i : i + 1, n * LANES : (n + 1) * LANES] = v[n : n + 1, :]
    t_out[...] = state[0:K, 0:K]


def swap(value, axes):
    return lax.all_to_all(value, axes, 0, 0, tiled=True)


def swap_across(value):
    place_of = lambda x, k, z, y: ((x * NCORE + k) * NZ + z) * NY + y
    groups = [
        [place_of(x, (k + far(x)) % NCORE, z, y) for x in range(NX) for y in range(NY)]
        for k in range(NCORE)
        for z in range(NZ)
    ]
    return lax.all_to_all(value, ("x", "core", "z", "y"), 0, 0, axis_index_groups=groups, tiled=True)


def call(kernel, ins, outs, scratch=(), mib=8, **more):
    return pl.pallas_call(
        kernel,
        in_specs=[VMEM] * len(ins),
        out_specs=[VMEM] * len(outs),
        out_shape=[vec(*shape) for shape in outs],
        scratch_shapes=[pltpu.VMEM(shape, f32) for shape in scratch],
        compiler_params=params(mib),
        **more,
    )(*ins)


def spread_panel(matrix):
    cols, sent = pl.pallas_call(
        take_panel,
        in_specs=[pl.BlockSpec(memory_space=pl.ANY)],
        out_specs=[VMEM] * 2,
        out_shape=[vec(K, BLOCK, LANES), vec(NX * NCORE, BLOCK, LANES)],
        scratch_shapes=[pltpu.VMEM((matrix.shape[0], LANES), f32), pltpu.SemaphoreType.DMA((CHUNKS,))],
        compiler_params=params(48),
    )(matrix)
    return call(
        pack_panel,
        [swap(sent, ("x", "core")), cols],
        [(NZ * NY, 1, (WIDE + SLICE) * LANES)],
    )[0]


def on_device(matrix):
    rows_dev, cols_dev = matrix.shape

    sent = lax.cond(
        (lax.axis_index("z") == 0) & (lax.axis_index("y") == 0),
        spread_panel,
        lambda _: jnp.zeros((NZ * NY, 1, (WIDE + SLICE) * LANES), f32),
        matrix,
    )
    (mine,) = call(
        pick_panel,
        [swap(sent, ("z", "y"))],
        [(16, LANES)],
        cost_estimate=pl.CostEstimate(flops=1 << 32, bytes_accessed=1 << 20, transcendentals=0),
    )
    (sent,) = call(first_step, [mine, matrix], [(NZ, 32, LANES)], [(BLOCK, LANES)])
    (sent,) = call(pass_first, [swap(sent, "z")], [(GROUP, 2 * BLOCK, LANES)], [(2 * BLOCK, LANES)])
    mine, later = call(
        pick_first, [swap(sent, ("x", "y"))], [(3 * NX * BLOCK, LANES), (2 * NX * BLOCK, LANES)]
    )
    state, vs, ys = [], [], []
    for j in range(1, K):
        got = lax.all_gather(mine, "core")
        send = (NY if j == K - 1 else NZ, BLOCK, LANES)
        whole = (FULL, LANES)
        v, s, sent, y, *first = call(
            functools.partial(step, j),
            [got, matrix, *state, *vs, *ys],
            [whole, (8, LANES), send, whole] + [whole] * (j == 1),
            [whole, (BLOCK, LANES)],
        )
        state, vs, ys = [s], [*first, *vs, v], [*ys, y]
        if j < K - 1:
            (sent,) = call(pass_product, [swap(sent, "z")], [(GROUP, BLOCK, LANES)], [(BLOCK, LANES)])
            (mine,) = call(
                functools.partial(pick_product, j),
                [swap_across(sent), later],
                [(2 * NX * BLOCK, LANES)],
            )
    (sent,) = call(pass_product, [swap(sent, "y")], [(NZ, BLOCK, LANES)], [(BLOCK, LANES)])
    got = swap(sent, "z")
    return call(finish, [got, *state, *vs, *ys], [(K, rows_dev), (K, rows_dev), (K, K)])


def solution(mesh):
    grid = Mesh(mesh.devices.reshape(NX, NCORE, NZ, NY), ("x", "core", "z", "y"))
    return jax.shard_map(
        on_device,
        mesh=grid,
        in_specs=(P(("x", "core"), ("z", "y")),),
        out_specs=(P(None, ("x", "core")), P(None, ("x", "core")), P()),
        check_vma=False,
    )
```
